128 devices in a mesh: box: 16 (over z, x), dir: 8 (over y, core).
Axes of the slice: x: 4, y: 4, z: 4, core: 2. Of those that a mesh axis runs over, the one named last changes fastest.
Arguments:
- currents: bfloat16 [2048, 128, 128], P(('box', 'dir')), may hold values from -6 to 6
- near_blocks: bfloat16 [2048, 8, 128, 256], P(('box', 'dir')), may hold values from -0.375 to 0.375
- near_list: int32 [2048, 8], P(('box', 'dir')), may hold values from 0 to 2047, as said below
- near_count: int32 [2048], P(('box', 'dir')), may hold values from 2 to 8, as said below
- radiation: bfloat16 [1024, 256], replicated, may hold values from -0.375 to 0.375
- child_angle: float32 [2048, 1024], P(('box', 'dir')), may hold values from -3.140625 to 3.140625
- translation: float32 [316, 2, 1024], replicated, may hold values from -0.61237246 to 0.61237246
- inter_src: int32 [128, 6], replicated, may hold values from 0 to 127, as said below
- inter_off: int32 [128, 6], replicated, may hold values from 0 to 315
- inter_count: int32 [128], replicated, may hold values from 2 to 6, as said below
Outputs:
- field: bfloat16 [2048, 128, 128], P(('box', 'dir'))
The draws below stay inside these ranges and needn't reach their ends.
Inputs may be any that keep to these rules, and one draw needn't show every extreme that they name: `near_list`: entry k of leaf box b names a box at most 8 away from b; entry 0 is b itself and entry 1 lies exactly 8 away. Slots at or beyond near_count[b] of near_list and near_blocks are padding and are not used. `inter_src`: each row names 6 different upper-level boxes, none equal to the row's own. Only the first inter_count[p] slots of row p of inter_src and inter_off are used.
All inputs are finite; a program needn't handle non-finite values.
Results may differ from the reference program's by a relative error of at most 0.006.
Values may be sent and summed in bfloat16 or wider, within the bound.
A program may use at most 128 MiB of HBM per device.

```python
import jax
import jax.numpy as jnp
from jax import lax

P_SIZE = 128
R = 64
Q = 1024
CHILD = 16
BD = 16
KN = 8
KT = 6
NOFF = 316
REACH = 8
NB = 2048
NPAR = 128


def draw_near_list(key, part):
    box_ids = jnp.arange(NB, dtype=jnp.int32)[:, None]
    offsets = jax.random.randint(jax.random.fold_in(key, 11), (NB, KN), -REACH, REACH + 1).astype(jnp.int32)
    slot_ids = jnp.arange(KN, dtype=jnp.int32)[None, :]
    offsets = jnp.where(slot_ids == 0, 0, offsets)
    offsets = jnp.where(slot_ids == 1, REACH, offsets)
    target = box_ids + offsets
    outside = (target < 0) | (target >= NB)
    return jnp.where(outside, box_ids - offsets, target).astype(jnp.int32)


def draw_near_count(key, part):
    level = jax.random.randint(jax.random.fold_in(key, 21), (NB // BD,), KN // 2, KN + 1).astype(jnp.int32)
    level_box = jnp.repeat(level, BD)
    raw = jax.random.randint(jax.random.fold_in(key, 22), (NB,), 0, 2 ** 20).astype(jnp.int32)
    counts = raw % (level_box - 1) + 2
    chosen = jax.random.randint(jax.random.fold_in(key, 23), (), 0, NB)
    return counts.at[chosen].set(KN).astype(jnp.int32)


def draw_inter_src(key, part):
    raw = jax.random.randint(jax.random.fold_in(key, 31), (NPAR, NPAR), 0, 2 ** 16).astype(jnp.int32)
    scores = raw * NPAR + jnp.arange(NPAR, dtype=jnp.int32)[None, :]
    diagonal = jnp.arange(NPAR, dtype=jnp.int32)[:, None] == jnp.arange(NPAR, dtype=jnp.int32)[None, :]
    scores = jnp.where(diagonal, -1, scores)
    top_values, top_index = lax.top_k(scores, KT)
    return top_index.astype(jnp.int32)


def draw_inter_count(key, part):
    counts = jax.random.randint(jax.random.fold_in(key, 41), (NPAR,), 2, KT + 1).astype(jnp.int32)
    chosen = jax.random.randint(jax.random.fold_in(key, 42), (), 0, NPAR)
    return counts.at[chosen].set(KT).astype(jnp.int32)


def place_ends(entries, stream_key, smallest, high):
    longest = entries.shape.index(max(entries.shape))
    spots = []
    for shift in (0, 1):
        where = [jax.random.randint(jax.random.fold_in(stream_key, axis), (), 0, length) for axis, length in enumerate(entries.shape)]
        where[longest] = (where[longest] + shift) % entries.shape[longest]
        spots.append(tuple(where))
    return entries.at[spots[0]].set(smallest).at[spots[1]].set(high)


def block_levels(key, extent, pieces, low, largest):
    level = 1.0
    for dim, parts in pieces:
        steps = jax.random.uniform(jax.random.fold_in(jax.random.fold_in(key, 6), dim), (parts,), jnp.float32, low / len(pieces), largest / len(pieces))
        level = level * jnp.repeat(jnp.exp(steps), extent[dim] // parts).reshape((-1,) + (1,) * (len(extent) - 1 - dim))
    return level


def noise(stream_key, extent, scale, reach, cuts=(), kind=jnp.bfloat16):
    level = block_levels(stream_key, extent, cuts, -0.22, 0.18) if cuts else 1.0
    array = jax.random.normal(stream_key, extent, jnp.float32) * scale * level
    return jnp.minimum(jnp.maximum(array, -reach), reach).astype(kind)


def setup_inputs(seed: int = 0) -> dict:
    keys = jax.random.split(jax.random.key(seed), 11)
    currents = noise(keys[0], (NB, P_SIZE, 2 * R), 1.0, 6.0, ((0, 128),))
    near_blocks = noise(keys[1], (NB, KN, P_SIZE, 2 * P_SIZE), (2 * P_SIZE) ** -0.5, 0.375, ((0, 128),))
    near_list = draw_near_list(jax.random.fold_in(keys[10], 71), 0)
    near_count = draw_near_count(jax.random.fold_in(keys[10], 71), 0)
    radiation = noise(keys[4], (Q, 2 * P_SIZE), (2 * P_SIZE) ** -0.5, 0.375)
    child_angle = jnp.clip(jax.random.uniform(keys[5], (NB, Q), jnp.float32, -3.140625, 3.140625), -3.140625, 3.140625)
    translation = noise(keys[6], (NOFF, 2, Q), (1.0 / (KT * CHILD) ** 0.5), 0.61237246, (), jnp.float32)
    inter_src = draw_inter_src(jax.random.fold_in(keys[10], 71), 0)
    inter_off = place_ends(jax.random.randint(keys[8], (NPAR, KT), 0, NOFF), jax.random.fold_in(keys[8], 1), 0, NOFF - 1).astype(jnp.int32)
    inter_count = draw_inter_count(jax.random.fold_in(keys[10], 71), 0)
    return {"currents": currents, "near_blocks": near_blocks, "near_list": near_list, "near_count": near_count, "radiation": radiation, "child_angle": child_angle, "translation": translation, "inter_src": inter_src, "inter_off": inter_off, "inter_count": inter_count}


def stacked(field_rows):
    half_width = field_rows.shape[-1] // 2
    real_part = field_rows[..., :half_width]
    imag_part = field_rows[..., half_width:]
    lower_rows = jnp.concatenate([-imag_part, real_part], axis=-1)
    return jnp.concatenate([field_rows, lower_rows], axis=-2)


def reference(currents, near_blocks, near_list, near_count, radiation, child_angle, translation, inter_src, inter_off, inter_count):
    highest = lax.Precision.HIGHEST
    groups = NB // BD
    slot_ids = jnp.arange(KN, dtype=jnp.int32)

    def near_group(packed):
        group_blocks, group_list, group_count = packed
        neighbours = stacked(currents[group_list]).astype(jnp.float32)
        live_slot = (slot_ids[None, :] < group_count[:, None]).astype(jnp.float32)
        products = jnp.einsum("bkpj,bkjr->bkpr", group_blocks.astype(jnp.float32), neighbours, precision=highest)
        return jnp.sum(products * live_slot[:, :, None, None], axis=1)

    near_part = lax.map(near_group, (near_blocks.reshape(groups, BD, KN, P_SIZE, 2 * P_SIZE), near_list.reshape(groups, BD, KN), near_count.reshape(groups, BD)))
    near_part = near_part.reshape(NB, P_SIZE, 2 * R)

    rad_full = radiation.astype(jnp.float32)
    angles = child_angle.reshape(NPAR, CHILD, Q)

    def parent_pattern(packed):
        child_currents, child_phase = packed
        leaf_terms = jnp.einsum("qj,bjr->bqr", rad_full, stacked(child_currents).astype(jnp.float32), precision=highest)
        cos_part = jnp.cos(child_phase)[:, :, None]
        sin_part = jnp.sin(child_phase)[:, :, None]
        real_part = leaf_terms[..., :R]
        imag_part = leaf_terms[..., R:]
        return jnp.concatenate([jnp.sum(cos_part * real_part - sin_part * imag_part, axis=0), jnp.sum(sin_part * real_part + cos_part * imag_part, axis=0)], axis=-1)

    pattern = lax.map(parent_pattern, (currents.reshape(NPAR, CHILD, P_SIZE, 2 * R), angles)).astype(jnp.bfloat16)
    pattern_full = pattern.astype(jnp.float32)
    trans_ids = jnp.arange(KT, dtype=jnp.int32)

    def translate_one(packed):
        src_row, off_row, count_one = packed
        operators = translation[off_row]
        live_slot = (trans_ids < count_one).astype(jnp.float32)[:, None, None]
        real_op = operators[:, 0, :, None] * live_slot
        imag_op = operators[:, 1, :, None] * live_slot
        sources = pattern_full[src_row]
        real_part = sources[..., :R]
        imag_part = sources[..., R:]
        return jnp.concatenate([jnp.sum(real_op * real_part - imag_op * imag_part, axis=0), jnp.sum(real_op * imag_part + imag_op * real_part, axis=0)], axis=-1)

    incoming = lax.map(translate_one, (inter_src, inter_off, inter_count)).astype(jnp.bfloat16)

    def parent_field(packed):
        parent_in, child_phase = packed
        incoming_full = parent_in.astype(jnp.float32)[None]
        cos_part = jnp.cos(child_phase)[:, :, None]
        sin_part = jnp.sin(child_phase)[:, :, None]
        real_part = incoming_full[..., :R]
        imag_part = incoming_full[..., R:]
        shifted = jnp.concatenate([cos_part * real_part + sin_part * imag_part, cos_part * imag_part - sin_part * real_part], axis=-1).astype(jnp.bfloat16)
        mixed_terms = jnp.einsum("qj,bqr->bjr", rad_full, shifted.astype(jnp.float32), precision=highest)
        far_real = mixed_terms[:, :P_SIZE, :R] + mixed_terms[:, P_SIZE:, R:]
        far_imag = mixed_terms[:, :P_SIZE, R:] - mixed_terms[:, P_SIZE:, :R]
        return jnp.concatenate([far_real, far_imag], axis=-1)

    far_part = lax.map(parent_field, (incoming, angles)).reshape(NB, P_SIZE, 2 * R)
    return (near_part + far_part).astype(jnp.bfloat16)
```

```python
import functools

import jax
import jax.numpy as jnp
from jax import lax
from jax.experimental import pallas as pl
from jax.experimental.pallas import tpu as pltpu
from jax.sharding import PartitionSpec as P

MESH = pl.DeviceIdType.MESH
F32 = jnp.float32
BF16 = jnp.bfloat16
NT = (((1,), (1,)), ((), ()))


def sincos(angle):
    h = angle * 0.5
    z = h * h
    s = -1.0 / 1307674368000.0
    for inv in (6227020800.0, -39916800.0, 362880.0, -5040.0, 120.0, -6.0, 1.0):
        s = s * z + 1.0 / inv
    s = s * h
    c = 1.0 / 20922789888000.0
    for inv in (-87178291200.0, 479001600.0, -3628800.0, 40320.0, -720.0, 24.0, -2.0, 1.0):
        c = c * z + 1.0 / inv
    return 2.0 * s * c, 1.0 - 2.0 * s * s


def iota2(rows, columns):
    return (
        lax.broadcasted_iota(jnp.int32, (rows, columns), 0),
        lax.broadcasted_iota(jnp.int32, (rows, columns), 1),
    )


def kernel(
    nbox,
    ndir,
    ids,
    src,
    off,
    x_hbm,
    z_hbm,
    a_hbm,
    ang_hbm,
    tr_hbm,
    out_ref,
    xext,
    zbuf,
    a_ref,
    ang,
    trans,
    cosb,
    sinb,
    lhs,
    send1,
    recv1,
    recv2,
    send3,
    recv3,
    recv4,
    near,
    inc,
    shf,
    load_sem,
    own_sem,
    s1,
    r1,
    s2,
    r2,
    s3,
    r3,
    s4,
    r4,
    sh,
    rh,
):
    box = lax.axis_index("box")
    me = lax.axis_index("dir")
    chips = ndir // 2
    my_y = me // 2
    boxes = x_hbm.shape[0]
    half = boxes // 2

    rank = box * ndir + me
    total = nbox * ndir
    right = lax.rem(rank + 1, total)
    left = lax.rem(rank + total - 1, total)
    right_id = (right // ndir, lax.rem(right, ndir))
    left_id = (left // ndir, lax.rem(left, ndir))

    barrier = pltpu.get_barrier_semaphore()
    for s in range(1, ndir):
        pl.semaphore_signal(
            barrier, inc=1, device_id=(box, lax.rem(me + s, ndir)), device_id_type=MESH
        )
    for s in range(1, nbox):
        pl.semaphore_signal(
            barrier, inc=1, device_id=(lax.rem(box + s, nbox), me), device_id_type=MESH
        )
    for there in (left_id, right_id):
        pl.semaphore_signal(barrier, inc=1, device_id=there, device_id_type=MESH)

    load_x = pltpu.make_async_copy(x_hbm, xext.at[pl.ds(half, boxes)], load_sem.at[0])
    load_a = pltpu.make_async_copy(a_hbm, a_ref, load_sem.at[1])
    load_g = pltpu.make_async_copy(ang_hbm, ang, load_sem.at[2])
    load_t = pltpu.make_async_copy(
        tr_hbm.at[:, :, pl.ds(pl.multiple_of(me * 128, 128), 128)],
        trans.at[pl.ds(0, tr_hbm.shape[0])],
        load_sem.at[3],
    )
    load_z = pltpu.make_async_copy(z_hbm, zbuf, load_sem.at[4])
    load_x.start()
    load_g.start()
    load_a.start()
    load_t.start()
    load_z.start()

    xext[2 * boxes] = jnp.zeros((128, 128), BF16)
    trans[pl.ds(tr_hbm.shape[0], 4)] = jnp.zeros((4, 2, 128), F32)

    row, col = iota2(128, 128)
    within = lax.rem(row, 8)
    natural = 4 * lax.div(row, 8) + lax.rem(within, 4) + 64 * lax.div(within, 4)
    perm = jnp.where(col == natural, 1.0, 0.0).astype(BF16)
    within_t = lax.rem(col, 8)
    natural_t = 4 * lax.div(col, 8) + lax.rem(within_t, 4) + 64 * lax.div(within_t, 4)
    perm_t = jnp.where(row == natural_t, 1.0, 0.0).astype(BF16)
    row2, col2 = iota2(256, 128)
    spread = jnp.where(row2 == col2, 1.0, 0.0)
    spread = jnp.where((row2 >= 128) & (row2 < 192) & (col2 == row2 - 64), -1.0, spread)
    spread = jnp.where((row2 >= 192) & (col2 == row2 - 192), 1.0, spread).astype(BF16)

    load_g.wait()
    for y in range(chips):
        sn, cs = sincos(ang[:, y * 256 : (y + 1) * 256])
        sinb[y] = sn
        cosb[y] = cs

    load_x.wait()
    for i in range(boxes // 4):
        four = xext[half + 4 * i : half + 4 * i + 4].reshape(512, 128)
        turned = lax.dot_general(spread, four, NT, preferred_element_type=F32).astype(BF16)
        for j in range(4):
            rows = slice((4 * i + j) * 128, (4 * i + j + 1) * 128)
            lhs[rows, 0:128] = turned[0:128, j * 128 : (j + 1) * 128]
            lhs[rows, 128:256] = turned[128:256, j * 128 : (j + 1) * 128]

    load_a.wait()
    pl.semaphore_wait(barrier, ndir + nbox)

    def copy1(j):
        return pltpu.make_async_remote_copy(
            src_ref=send1.at[j],
            dst_ref=recv1.at[me],
            send_sem=s1.at[j],
            recv_sem=r1.at[me],
            device_id=(box, j),
            device_id_type=MESH,
        )

    def wait1(j):
        return pltpu.make_async_remote_copy(
            src_ref=send1.at[j],
            dst_ref=recv1.at[j],
            send_sem=s1.at[j],
            recv_sem=r1.at[j],
            device_id=(box, j),
            device_id_type=MESH,
        )

    own1 = pltpu.make_async_copy(send1.at[me], recv1.at[me], own_sem.at[0])

    def pattern_step(s, carry):
        y = lax.rem(my_y + 1 + s, chips)
        block = a_ref[pl.ds(pl.multiple_of(y * 256, 256), 256), :]
        re = jnp.zeros((64, 256), F32)
        im = jnp.zeros((64, 256), F32)
        for i in range(boxes // 4):
            terms = lax.dot_general(
                lhs[512 * i : 512 * (i + 1), :], block, NT, preferred_element_type=F32
            )
            for j in range(4):
                b = 4 * i + j
                c = cosb[y, b : b + 1, :]
                d = sinb[y, b : b + 1, :]
                tre = terms[j * 128 : j * 128 + 64]
                tim = terms[j * 128 + 64 : (j + 1) * 128]
                re = re + (c * tre - d * tim)
                im = im + (d * tre + c * tim)
        pat = jnp.concatenate([re, im], axis=0).astype(BF16)
        pat = jnp.dot(perm, pat, preferred_element_type=F32)
        for h in range(2):
            j = 2 * y + h
            send1[j] = pat[:, h * 128 : (h + 1) * 128].reshape(nbox, 8, 128).astype(BF16)

            @pl.when(j != me)
            def _():
                copy1(j).start()

            @pl.when(j == me)
            def _():
                own1.start()

        return carry

    lax.fori_loop(0, chips, pattern_step, 0)

    to_right = pltpu.make_async_remote_copy(
        src_ref=xext.at[pl.ds(boxes, half)],
        dst_ref=xext.at[pl.ds(0, half)],
        send_sem=sh.at[0],
        recv_sem=rh.at[0],
        device_id=right_id,
        device_id_type=MESH,
    )
    to_left = pltpu.make_async_remote_copy(
        src_ref=xext.at[pl.ds(half, half)],
        dst_ref=xext.at[pl.ds(half + boxes, half)],
        send_sem=sh.at[1],
        recv_sem=rh.at[1],
        device_id=left_id,
        device_id_type=MESH,
    )

    own1.wait()
    for s in range(1, ndir):
        wait1(lax.rem(me + s, ndir)).wait_recv()

    def copy2(g, slot):
        return pltpu.make_async_remote_copy(
            src_ref=recv1.at[:, g],
            dst_ref=recv2.at[pl.ds(slot * 8, 8)],
            send_sem=s2.at[g],
            recv_sem=r2.at[slot],
            device_id=(g, me),
            device_id_type=MESH,
        )

    own2 = pltpu.make_async_copy(recv1.at[:, box], recv2.at[pl.ds(box * 8, 8)], own_sem.at[1])
    for s in range(1, nbox):
        copy2(lax.rem(box + s, nbox), box).start()
    own2.start()
    to_right.start()
    to_left.start()

    load_t.wait()
    own2.wait()
    for s in range(1, nbox):
        g = lax.rem(box + s, nbox)
        copy2(g, g).wait_recv()

    def copy3(g, slot):
        return pltpu.make_async_remote_copy(
            src_ref=send3.at[pl.ds(g * 8, 8)],
            dst_ref=recv3.at[slot],
            send_sem=s3.at[g],
            recv_sem=r3.at[slot],
            device_id=(g, me),
            device_id_type=MESH,
        )

    own3 = pltpu.make_async_copy(send3.at[pl.ds(box * 8, 8)], recv3.at[box], own_sem.at[2])
    sign = jnp.where(lax.broadcasted_iota(jnp.int32, (8, 128), 0) < 4, -1.0, 1.0)
    slots = src.shape[0] // (nbox * ndir)

    def translate_step(s, carry):
        g = lax.rem(box + 1 + s, nbox)
        for i in range(ndir):
            t = g * ndir + i
            straight = jnp.zeros((8, 128), F32)
            crossed = jnp.zeros((8, 128), F32)
            for k in range(slots):
                v = recv2[src[t * slots + k]].astype(F32)
                tau = trans[off[t * slots + k]]
                straight = straight + tau[0:1] * v
                crossed = crossed + tau[1:2] * v
            total_in = straight + sign * pltpu.roll(crossed, 4, 0)
            send3[t] = total_in.astype(BF16)

        @pl.when(g != box)
        def _():
            copy3(g, box).start()

        @pl.when(g == box)
        def _():
            own3.start()

        return carry

    lax.fori_loop(0, nbox, translate_step, 0)

    load_z.wait()
    to_right.wait_recv()
    to_left.wait_recv()

    def near_step(b, carry):
        gathered = jnp.concatenate([xext[ids[b * 8 + k]] for k in range(8)], axis=0)
        zr = jnp.concatenate([zbuf[b, k, :, 0:128] for k in range(8)], axis=1)
        zi = jnp.concatenate([zbuf[b, k, :, 128:256] for k in range(8)], axis=1)
        both = jnp.dot(
            jnp.concatenate([zr, zi], axis=0), gathered, preferred_element_type=F32
        )
        cross = pltpu.roll(both[128:256], 64, 1)
        lane = lax.broadcasted_iota(jnp.int32, (128, 128), 1)
        near[b] = both[0:128] + jnp.where(lane < 64, -cross, cross)
        return carry

    lax.fori_loop(0, boxes, near_step, 0)

    own3.wait()
    for s in range(1, nbox):
        g = lax.rem(box + s, nbox)
        copy3(g, g).wait_recv()

    def copy4(j, slot):
        return pltpu.make_async_remote_copy(
            src_ref=recv3.at[:, j],
            dst_ref=recv4.at[slot],
            send_sem=s4.at[j],
            recv_sem=r4.at[slot],
            device_id=(box, j),
            device_id_type=MESH,
        )

    own4 = pltpu.make_async_copy(recv3.at[:, me], recv4.at[me], own_sem.at[3])
    for s in range(1, ndir):
        copy4(lax.rem(me + s, ndir), me).start()
    own4.start()
    own4.wait()
    for s in range(1, ndir):
        j = lax.rem(me + s, ndir)
        copy4(j, j).wait_recv()

    for y in range(chips):
        pair = jnp.concatenate(
            [recv4[2 * y + h].astype(F32).reshape(128, 128).astype(BF16) for h in range(2)], axis=1
        )
        inc[:, y * 256 : (y + 1) * 256] = jnp.dot(perm_t, pair, preferred_element_type=F32)

    def far_step(i, carry):
        for j in range(4):
            b = 4 * i + j
            for y in range(chips):
                lanes = slice(y * 256, (y + 1) * 256)
                c = cosb[y, pl.ds(b, 1), :]
                d = sinb[y, pl.ds(b, 1), :]
                re = inc[0:64, lanes]
                im = inc[64:128, lanes]
                shf[j * 128 : j * 128 + 64, lanes] = (c * re + d * im).astype(BF16)
                shf[j * 128 + 64 : (j + 1) * 128, lanes] = (c * im - d * re).astype(BF16)
        mixed = jnp.dot(shf[...], a_ref[...], preferred_element_type=F32)
        for j in range(4):
            b = 4 * i + j
            m = mixed[j * 128 : (j + 1) * 128]
            far = jnp.concatenate(
                [m[0:64, 0:128] + m[64:128, 128:256], m[64:128, 0:128] - m[0:64, 128:256]], axis=0
            )
            out_ref[b] = (near[b] + far.T).astype(BF16)
        return carry

    lax.fori_loop(0, boxes // 4, far_step, 0)

    to_right.wait_send()
    to_left.wait_send()
    for s in range(1, ndir):
        j = lax.rem(me + s, ndir)
        copy1(j).wait_send()
        copy4(j, me).wait_send()
    for s in range(1, nbox):
        g = lax.rem(box + s, nbox)
        copy2(g, box).wait_send()
        copy3(g, box).wait_send()


def local(
    nbox,
    ndir,
    currents,
    near_blocks,
    near_list,
    near_count,
    radiation,
    child_angle,
    translation,
    inter_src,
    inter_off,
    inter_count,
):
    boxes = currents.shape[0]
    half = boxes // 2
    kn = near_list.shape[1]
    slots = inter_src.shape[1]
    first = (lax.axis_index("box") * ndir + lax.axis_index("dir")) * boxes
    live = jnp.arange(kn, dtype=jnp.int32)[None, :] < near_count[:, None]
    ids = jnp.where(live, jnp.clip(near_list - first + half, 0, 2 * boxes - 1), 2 * boxes)
    used = jnp.arange(slots, dtype=jnp.int32)[None, :] < inter_count[:, None]
    offs = jnp.where(used, jnp.clip(inter_off, 0, translation.shape[0] - 1), translation.shape[0])
    srcs = jnp.clip(inter_src, 0, nbox * ndir - 1)
    smem = pl.BlockSpec(memory_space=pltpu.SMEM)
    hbm = pl.BlockSpec(memory_space=pl.ANY)
    dma = pltpu.SemaphoreType.DMA
    return pl.pallas_call(
        functools.partial(kernel, nbox, ndir),
        out_shape=jax.ShapeDtypeStruct((boxes, 128, 128), BF16),
        in_specs=[smem] * 3 + [hbm] * 5,
        out_specs=pl.BlockSpec(memory_space=pltpu.VMEM),
        scratch_shapes=[
            pltpu.VMEM((2 * boxes + 1, 128, 128), BF16),
            pltpu.VMEM(near_blocks.shape, BF16),
            pltpu.VMEM(radiation.shape, BF16),
            pltpu.VMEM(child_angle.shape, F32),
            pltpu.VMEM((translation.shape[0] + 4, 2, 128), F32),
            pltpu.VMEM((ndir // 2, boxes, 256), F32),
            pltpu.VMEM((ndir // 2, boxes, 256), F32),
            pltpu.VMEM((boxes * 128, 256), BF16),
            pltpu.VMEM((ndir, nbox, 8, 128), BF16),
            pltpu.VMEM((ndir, nbox, 8, 128), BF16),
            pltpu.VMEM((nbox * ndir, 8, 128), BF16),
            pltpu.VMEM((nbox * ndir, 8, 128), BF16),
            pltpu.VMEM((nbox, ndir, 8, 128), BF16),
            pltpu.VMEM((ndir, nbox, 8, 128), BF16),
            pltpu.VMEM((boxes, 128, 128), F32),
            pltpu.VMEM((128, ndir * 128), F32),
            pltpu.VMEM((512, ndir * 128), BF16),
            dma((5,)),
            dma((4,)),
            dma((ndir,)),
            dma((ndir,)),
            dma((nbox,)),
            dma((nbox,)),
            dma((nbox,)),
            dma((nbox,)),
            dma((ndir,)),
            dma((ndir,)),
            dma((2,)),
            dma((2,)),
        ],
        compiler_params=pltpu.CompilerParams(
            collective_id=0, has_side_effects=True, vmem_limit_bytes=50 * 2**20
        ),
    )(
        ids.reshape(-1),
        srcs.reshape(-1),
        offs.reshape(-1),
        currents,
        near_blocks,
        radiation,
        child_angle,
        translation,
    )


def solution(mesh):
    nbox, ndir = mesh.shape["box"], mesh.shape["dir"]
    return jax.shard_map(
        functools.partial(local, nbox, ndir),
        mesh=mesh,
        in_specs=(
            P(("box", "dir"), None, None),
            P(("box", "dir"), None, None, None),
            P(("box", "dir"), None),
            P(("box", "dir")),
            P(),
            P(("box", "dir"), None),
            P(),
            P(),
            P(),
            P(),
        ),
        out_specs=P(("box", "dir"), None, None),
        check_vma=False,
    )
```

```python
import functools

import jax
import jax.numpy as jnp
from jax import lax
from jax.experimental import pallas as pl
from jax.experimental.pallas import tpu as pltpu
from jax.sharding import PartitionSpec as P

LOGICAL = pl.DeviceIdType.LOGICAL
F32 = jnp.float32
BF16 = jnp.bfloat16
NT = (((1,), (1,)), ((), ()))


def sincos(angle):
    h = angle * 0.5
    z = h * h
    s = -1.0 / 1307674368000.0
    for inv in (6227020800.0, -39916800.0, 362880.0, -5040.0, 120.0, -6.0, 1.0):
        s = s * z + 1.0 / inv
    s = s * h
    c = 1.0 / 20922789888000.0
    for inv in (-87178291200.0, 479001600.0, -3628800.0, 40320.0, -720.0, 24.0, -2.0, 1.0):
        c = c * z + 1.0 / inv
    return 2.0 * s * c, 1.0 - 2.0 * s * s


def iota2(rows, columns):
    return (
        lax.broadcasted_iota(jnp.int32, (rows, columns), 0),
        lax.broadcasted_iota(jnp.int32, (rows, columns), 1),
    )


def kernel(
    nbox,
    ndir,
    list_hbm,
    count_hbm,
    src_hbm,
    off_hbm,
    used_hbm,
    x_hbm,
    z_hbm,
    a_hbm,
    ang_hbm,
    tr_hbm,
    out_hbm,
    nlist,
    ncount,
    src,
    off,
    used,
    xext,
    zbuf,
    a_ref,
    ang,
    trans,
    cosb,
    sinb,
    lhs,
    send1,
    recv1,
    send2,
    recv2,
    near,
    inc,
    shf,
    out,
    load_sem,
    table_sem,
    own_sem,
    out_sem,
    s1,
    r1,
    s2,
    r2,
    sh,
    rh,
):
    box = lax.axis_index("box")
    me = lax.axis_index("dir")
    chips = ndir // 2
    my_y = me // 2
    boxes = x_hbm.shape[0]
    half = boxes // 2
    total = nbox * ndir
    rank = box * ndir + me

    load_x = pltpu.make_async_copy(x_hbm, xext.at[pl.ds(half, boxes)], load_sem.at[0])
    load_a = pltpu.make_async_copy(a_hbm, a_ref, load_sem.at[1])
    load_g = pltpu.make_async_copy(ang_hbm, ang, load_sem.at[2])
    load_t = pltpu.make_async_copy(
        tr_hbm.at[:, :, pl.ds(pl.multiple_of(me * 128, 128), 128)],
        trans.at[pl.ds(0, tr_hbm.shape[0])],
        load_sem.at[3],
    )
    load_z = pltpu.make_async_copy(z_hbm, zbuf, load_sem.at[4])
    tables = [
        pltpu.make_async_copy(there, here, table_sem.at[i])
        for i, (there, here) in enumerate(
            (
                (list_hbm, nlist),
                (count_hbm, ncount),
                (src_hbm, src),
                (off_hbm, off),
                (used_hbm, used),
            )
        )
    ]
    load_g.start()
    load_x.start()
    load_a.start()
    load_t.start()
    for table in tables:
        table.start()
    load_z.start()

    barrier = pltpu.get_barrier_semaphore()
    for s in range(1, total):
        pl.semaphore_signal(
            barrier,
            inc=1,
            device_id=lax.rem(rank + s, total),
            device_id_type=LOGICAL,
        )

    xext[2 * boxes] = jnp.zeros((128, 128), BF16)
    trans[pl.ds(tr_hbm.shape[0], 4)] = jnp.zeros((4, 2, 128), F32)

    row, col = iota2(128, 128)
    within = lax.rem(row, 8)
    natural = 4 * lax.div(row, 8) + lax.rem(within, 4) + 64 * lax.div(within, 4)
    perm = jnp.where(col == natural, 1.0, 0.0).astype(BF16)
    within_t = lax.rem(col, 8)
    natural_t = 4 * lax.div(col, 8) + lax.rem(within_t, 4) + 64 * lax.div(within_t, 4)
    perm_t = jnp.where(row == natural_t, 1.0, 0.0).astype(BF16)
    row2, col2 = iota2(256, 128)
    spread = jnp.where(row2 == col2, 1.0, 0.0)
    spread = jnp.where((row2 >= 128) & (row2 < 192) & (col2 == row2 - 64), -1.0, spread)
    spread = jnp.where((row2 >= 192) & (col2 == row2 - 192), 1.0, spread).astype(BF16)

    load_g.wait()
    for y in range(chips):
        sn, cs = sincos(ang[:, y * 256 : (y + 1) * 256])
        sinb[y] = sn
        cosb[y] = cs

    load_x.wait()
    for i in range(boxes // 4):
        four = xext[half + 4 * i : half + 4 * i + 4].reshape(512, 128)
        turned = lax.dot_general(spread, four, NT, preferred_element_type=F32).astype(BF16)
        for j in range(4):
            rows = slice((4 * i + j) * 128, (4 * i + j + 1) * 128)
            lhs[rows, 0:128] = turned[0:128, j * 128 : (j + 1) * 128]
            lhs[rows, 128:256] = turned[128:256, j * 128 : (j + 1) * 128]

    load_a.wait()

    own1 = pltpu.make_async_copy(send1.at[me * nbox + box], recv1.at[rank], own_sem.at[0])

    def pattern_step(s, carry):
        y = lax.rem(my_y + 1 + s, chips)
        block = a_ref[pl.ds(pl.multiple_of(y * 256, 256), 256), :]
        re = jnp.zeros((64, 256), F32)
        im = jnp.zeros((64, 256), F32)
        for i in range(boxes // 4):
            terms = lax.dot_general(
                lhs[512 * i : 512 * (i + 1), :], block, NT, preferred_element_type=F32
            )
            for j in range(4):
                b = 4 * i + j
                c = cosb[y, b : b + 1, :]
                d = sinb[y, b : b + 1, :]
                tre = terms[j * 128 : j * 128 + 64]
                tim = terms[j * 128 + 64 : (j + 1) * 128]
                re = re + (c * tre - d * tim)
                im = im + (d * tre + c * tim)
        pat = jnp.concatenate([re, im], axis=0).astype(BF16)
        pat = jnp.dot(perm, pat, preferred_element_type=F32)
        for h in range(2):
            send1[pl.ds((2 * y + h) * nbox, nbox)] = (
                pat[:, h * 128 : (h + 1) * 128].reshape(nbox, 8, 128).astype(BF16)
            )

        @pl.when(s == 0)
        def _():
            pl.semaphore_wait(barrier, total - 1)

        def send(g, j):
            pltpu.make_async_remote_copy(
                src_ref=send1.at[j * nbox + g],
                dst_ref=recv1.at[rank],
                send_sem=s1,
                recv_sem=r1,
                device_id=g * ndir + j,
                device_id_type=LOGICAL,
            ).start()

        for i in range(1, nbox):
            for h in range(2):
                send(lax.rem(box + i, nbox), 2 * y + h)
        for h in range(2):
            j = 2 * y + h

            @pl.when(j != me)
            def _():
                send(box, j)

            @pl.when(j == me)
            def _():
                own1.start()

        return carry

    lax.fori_loop(0, chips, pattern_step, 0)

    to_right = pltpu.make_async_remote_copy(
        src_ref=xext.at[pl.ds(boxes, half)],
        dst_ref=xext.at[pl.ds(0, half)],
        send_sem=sh.at[0],
        recv_sem=rh.at[0],
        device_id=lax.rem(rank + 1, total),
        device_id_type=LOGICAL,
    )
    to_left = pltpu.make_async_remote_copy(
        src_ref=xext.at[pl.ds(half, half)],
        dst_ref=xext.at[pl.ds(half + boxes, half)],
        send_sem=sh.at[1],
        recv_sem=rh.at[1],
        device_id=lax.rem(rank + total - 1, total),
        device_id_type=LOGICAL,
    )
    to_right.start()
    to_left.start()

    def all_but_one(there, here, send_sem, recv_sem):
        return pltpu.make_async_remote_copy(
            src_ref=there.at[pl.ds(0, total - 1)],
            dst_ref=here.at[pl.ds(0, total - 1)],
            send_sem=send_sem,
            recv_sem=recv_sem,
            device_id=lax.rem(rank + 1, total),
            device_id_type=LOGICAL,
        )

    load_t.wait()
    for table in tables:
        table.wait()
    own1.wait()
    all_but_one(send1, recv1, s1, r1).wait_recv()

    own2 = pltpu.make_async_copy(send2.at[rank], recv2.at[me * nbox + box], own_sem.at[1])
    sign = jnp.where(lax.broadcasted_iota(jnp.int32, (8, 128), 0) < 4, -1.0, 1.0)
    slots = src.shape[1]
    nothing = tr_hbm.shape[0]

    def translate_step(s, carry):
        g = lax.rem(box + 1 + s, nbox)
        for i in range(ndir):
            t = g * ndir + i
            straight = jnp.zeros((8, 128), F32)
            crossed = jnp.zeros((8, 128), F32)
            for k in range(slots):
                v = recv1[src[t, k]].astype(F32)
                tau = trans[jnp.where(k < used[t], off[t, k], nothing)]
                straight = straight + tau[0:1] * v
                crossed = crossed + tau[1:2] * v
            total_in = straight + sign * pltpu.roll(crossed, 4, 0)
            send2[t] = total_in.astype(BF16)

        for i in range(ndir):
            t = g * ndir + i

            @pl.when(t != rank)
            def _():
                pltpu.make_async_remote_copy(
                    src_ref=send2.at[t],
                    dst_ref=recv2.at[me * nbox + box],
                    send_sem=s2,
                    recv_sem=r2,
                    device_id=t,
                    device_id_type=LOGICAL,
                ).start()

            @pl.when(t == rank)
            def _():
                own2.start()

        return carry

    lax.fori_loop(0, nbox, translate_step, 0)

    load_z.wait()
    to_right.wait_recv()
    to_left.wait_recv()
    first = rank * boxes - half

    def near_step(b, carry):
        count = ncount[b]
        gathered = jnp.concatenate(
            [xext[jnp.where(k < count, nlist[b, k] - first, 2 * boxes)] for k in range(8)], axis=0
        )
        zr = jnp.concatenate([zbuf[b, k, :, 0:128] for k in range(8)], axis=1)
        zi = jnp.concatenate([zbuf[b, k, :, 128:256] for k in range(8)], axis=1)
        both = jnp.dot(
            jnp.concatenate([zr, zi], axis=0), gathered, preferred_element_type=F32
        )
        cross = pltpu.roll(both[128:256], 64, 1)
        lane = lax.broadcasted_iota(jnp.int32, (128, 128), 1)
        near[b] = both[0:128] + jnp.where(lane < 64, -cross, cross)
        return carry

    lax.fori_loop(0, boxes, near_step, 0)

    own2.wait()
    all_but_one(send2, recv2, s2, r2).wait_recv()

    for y in range(chips):
        pair = jnp.concatenate(
            [
                recv2[(2 * y + h) * nbox : (2 * y + h + 1) * nbox]
                .astype(F32)
                .reshape(128, 128)
                .astype(BF16)
                for h in range(2)
            ],
            axis=1,
        )
        inc[:, y * 256 : (y + 1) * 256] = jnp.dot(perm_t, pair, preferred_element_type=F32)

    def write(i):
        group = pl.ds(4 * i, 4)
        return pltpu.make_async_copy(out.at[group], out_hbm.at[group], out_sem.at[i])

    def far_step(i, carry):
        for j in range(4):
            b = 4 * i + j
            for y in range(chips):
                lanes = slice(y * 256, (y + 1) * 256)
                c = cosb[y, pl.ds(b, 1), :]
                d = sinb[y, pl.ds(b, 1), :]
                re = inc[0:64, lanes]
                im = inc[64:128, lanes]
                shf[j * 128 : j * 128 + 64, lanes] = (c * re + d * im).astype(BF16)
                shf[j * 128 + 64 : (j + 1) * 128, lanes] = (c * im - d * re).astype(BF16)
        mixed = jnp.dot(shf[...], a_ref[...], preferred_element_type=F32)
        for j in range(4):
            b = 4 * i + j
            m = mixed[j * 128 : (j + 1) * 128]
            far = jnp.concatenate(
                [m[0:64, 0:128] + m[64:128, 128:256], m[64:128, 0:128] - m[0:64, 128:256]], axis=0
            )
            out[b] = (near[b] + far.T).astype(BF16)
        write(i).start()
        return carry

    lax.fori_loop(0, boxes // 4, far_step, 0)

    to_right.wait_send()
    to_left.wait_send()
    all_but_one(send1, recv1, s1, r1).wait_send()
    all_but_one(send2, recv2, s2, r2).wait_send()
    for i in range(boxes // 4):
        write(i).wait()


def local(
    nbox,
    ndir,
    currents,
    near_blocks,
    near_list,
    near_count,
    radiation,
    child_angle,
    translation,
    inter_src,
    inter_off,
    inter_count,
):
    boxes = currents.shape[0]
    total = nbox * ndir
    hbm = pl.BlockSpec(memory_space=pl.ANY)
    dma = pltpu.SemaphoreType.DMA
    return pl.pallas_call(
        functools.partial(kernel, nbox, ndir),
        out_shape=jax.ShapeDtypeStruct((boxes, 128, 128), BF16),
        in_specs=[hbm] * 10,
        out_specs=hbm,
        scratch_shapes=[
            pltpu.SMEM(near_list.shape, jnp.int32),
            pltpu.SMEM(near_count.shape, jnp.int32),
            pltpu.SMEM(inter_src.shape, jnp.int32),
            pltpu.SMEM(inter_off.shape, jnp.int32),
            pltpu.SMEM(inter_count.shape, jnp.int32),
            pltpu.VMEM((2 * boxes + 1, 128, 128), BF16),
            pltpu.VMEM(near_blocks.shape, BF16),
            pltpu.VMEM(radiation.shape, BF16),
            pltpu.VMEM(child_angle.shape, F32),
            pltpu.VMEM((translation.shape[0] + 4, 2, 128), F32),
            pltpu.VMEM((ndir // 2, boxes, 256), F32),
            pltpu.VMEM((ndir // 2, boxes, 256), F32),
            pltpu.VMEM((boxes * 128, 256), BF16),
            pltpu.VMEM((total, 8, 128), BF16),
            pltpu.VMEM((total, 8, 128), BF16),
            pltpu.VMEM((total, 8, 128), BF16),
            pltpu.VMEM((total, 8, 128), BF16),
            pltpu.VMEM((boxes, 128, 128), F32),
            pltpu.VMEM((128, ndir * 128), F32),
            pltpu.VMEM((512, ndir * 128), BF16),
            pltpu.VMEM((boxes, 128, 128), BF16),
            dma((5,)),
            dma((5,)),
            dma((2,)),
            dma((boxes // 4,)),
            dma,
            dma,
            dma,
            dma,
            dma((2,)),
            dma((2,)),
        ],
        compiler_params=pltpu.CompilerParams(
            collective_id=0, has_side_effects=True, vmem_limit_bytes=60 * 2**20
        ),
    )(
        near_list,
        near_count,
        inter_src,
        inter_off,
        inter_count,
        currents,
        near_blocks,
        radiation,
        child_angle,
        translation,
    )


def solution(mesh):
    nbox, ndir = mesh.shape["box"], mesh.shape["dir"]
    return jax.shard_map(
        functools.partial(local, nbox, ndir),
        mesh=mesh,
        in_specs=(
            P(("box", "dir"), None, None),
            P(("box", "dir"), None, None, None),
            P(("box", "dir"), None),
            P(("box", "dir")),
            P(),
            P(("box", "dir"), None),
            P(),
            P(),
            P(),
            P(),
        ),
        out_specs=P(("box", "dir"), None, None),
        check_vma=False,
    )
```

```python
import functools

import jax
import jax.numpy as jnp
from jax import lax
from jax.experimental import pallas as pl
from jax.experimental.pallas import tpu as pltpu
from jax.sharding import PartitionSpec as P

LOGICAL = pl.DeviceIdType.LOGICAL
F32 = jnp.float32
BF16 = jnp.bfloat16
NT = (((1,), (1,)), ((), ()))


def sincos(angle):
    h = angle * 0.5
    z = h * h
    s = -1.0 / 1307674368000.0
    for inv in (6227020800.0, -39916800.0, 362880.0, -5040.0, 120.0, -6.0, 1.0):
        s = s * z + 1.0 / inv
    s = s * h
    c = 1.0 / 20922789888000.0
    for inv in (-87178291200.0, 479001600.0, -3628800.0, 40320.0, -720.0, 24.0, -2.0, 1.0):
        c = c * z + 1.0 / inv
    return 2.0 * s * c, 1.0 - 2.0 * s * s


def far_groups(side):
    return sorted(
        ((z, x) for z in range(side) for x in range(side)),
        key=lambda o: -min(o[0], side - o[0]) - min(o[1], side - o[1]),
    )


def iota2(rows, columns):
    return (
        lax.broadcasted_iota(jnp.int32, (rows, columns), 0),
        lax.broadcasted_iota(jnp.int32, (rows, columns), 1),
    )


def kernel(
    nbox,
    ndir,
    list_hbm,
    count_hbm,
    src_hbm,
    off_hbm,
    used_hbm,
    x_hbm,
    z_hbm,
    a_hbm,
    ang_hbm,
    tr_hbm,
    out,
    nlist,
    ncount,
    src,
    off,
    used,
    xsib,
    xoth,
    zbuf,
    a_ref,
    ang,
    trans,
    cosb,
    sinb,
    lhs,
    send1,
    recv1,
    send2,
    recv2,
    near,
    inc,
    shf,
    load_sem,
    table_sem,
    own_sem,
    s1,
    r1,
    s2,
    r2,
    sh,
    rh,
):
    box = lax.axis_index("box")
    me = lax.axis_index("dir")
    chips = ndir // 2
    side = round(nbox**0.5)
    box_z, box_x = box // side, lax.rem(box, side)

    def group_at(offset):
        return lax.rem(box_z + offset[0], side) * side + lax.rem(box_x + offset[1], side)

    my_y = me // 2
    core = lax.rem(me, 2)
    boxes = x_hbm.shape[0]
    half = boxes // 2
    total = nbox * ndir
    rank = box * ndir + me

    barrier = pltpu.get_barrier_semaphore()
    for there in range(1, total):
        pl.semaphore_signal(
            barrier,
            inc=1,
            device_id=lax.rem(rank + there, total),
            device_id_type=LOGICAL,
        )

    load_x = pltpu.make_async_copy(x_hbm, xsib.at[pl.ds(core * half, boxes)], load_sem.at[0])
    load_o = pltpu.make_async_copy(x_hbm, xoth.at[pl.ds((1 - core) * half, boxes)], load_sem.at[5])
    load_a = pltpu.make_async_copy(a_hbm, a_ref, load_sem.at[1])
    load_g = pltpu.make_async_copy(ang_hbm, ang, load_sem.at[2])
    load_t = pltpu.make_async_copy(
        tr_hbm.at[:, :, pl.ds(pl.multiple_of(me * 128, 128), 128)],
        trans.at[pl.ds(0, tr_hbm.shape[0])],
        load_sem.at[3],
    )
    load_z = pltpu.make_async_copy(z_hbm, zbuf, load_sem.at[4])
    tables = [
        pltpu.make_async_copy(there, here, table_sem.at[i])
        for i, (there, here) in enumerate(
            (
                (list_hbm, nlist),
                (count_hbm, ncount),
                (src_hbm, src),
                (off_hbm, off),
                (used_hbm, used),
            )
        )
    ]
    load_g.start()
    load_x.start()
    load_a.start()
    load_o.start()
    load_t.start()
    for table in tables:
        table.start()
    load_z.start()

    xsib[boxes + half] = jnp.zeros((128, 128), BF16)
    xoth[boxes + half] = jnp.zeros((128, 128), BF16)
    trans[pl.ds(tr_hbm.shape[0], 4)] = jnp.zeros((4, 2, 128), F32)

    row, col = iota2(128, 128)
    within = lax.rem(row, 8)
    natural = 4 * lax.div(row, 8) + lax.rem(within, 4) + 64 * lax.div(within, 4)
    perm = jnp.where(col == natural, 1.0, 0.0).astype(BF16)
    within_t = lax.rem(col, 8)
    natural_t = 4 * lax.div(col, 8) + lax.rem(within_t, 4) + 64 * lax.div(within_t, 4)
    perm_t = jnp.where(row == natural_t, 1.0, 0.0).astype(BF16)
    row2, col2 = iota2(256, 128)
    spread = jnp.where(row2 == col2, 1.0, 0.0)
    spread = jnp.where((row2 >= 128) & (row2 < 192) & (col2 == row2 - 64), -1.0, spread)
    spread = jnp.where((row2 >= 192) & (col2 == row2 - 192), 1.0, spread).astype(BF16)

    load_g.wait()
    for y in range(chips):
        sn, cs = sincos(ang[:, y * 256 : (y + 1) * 256])
        sinb[y] = sn
        cosb[y] = cs

    load_x.wait()
    for i in range(boxes // 4):
        four = xsib[pl.ds(core * half + 4 * i, 4)].reshape(512, 128)
        turned = lax.dot_general(spread, four, NT, preferred_element_type=F32).astype(BF16)
        for j in range(4):
            rows = slice((4 * i + j) * 128, (4 * i + j + 1) * 128)
            lhs[rows, 0:128] = turned[0:128, j * 128 : (j + 1) * 128]
            lhs[rows, 128:256] = turned[128:256, j * 128 : (j + 1) * 128]

    load_a.wait()
    load_o.wait()

    own1 = pltpu.make_async_copy(send1.at[me * nbox + box], recv1.at[rank], own_sem.at[0])

    to_sibling = pltpu.make_async_remote_copy(
        src_ref=xsib.at[pl.ds(half, half)],
        dst_ref=xsib.at[pl.ds(core * boxes, half)],
        send_sem=sh.at[0],
        recv_sem=rh.at[0],
        device_id=rank + 1 - 2 * core,
        device_id_type=LOGICAL,
    )
    to_other = pltpu.make_async_remote_copy(
        src_ref=xoth.at[pl.ds(half, half)],
        dst_ref=xoth.at[pl.ds((1 - core) * boxes, half)],
        send_sem=sh.at[1],
        recv_sem=rh.at[1],
        device_id=lax.rem(rank + total - 1 + 2 * core, total),
        device_id_type=LOGICAL,
    )

    def pattern_step(s, carry):
        y = lax.rem(my_y + jnp.where(s == 0, 2, jnp.where(s == 1, 1, jnp.where(s == 2, 3, 0))), chips)
        block = a_ref[pl.ds(pl.multiple_of(y * 256, 256), 256), :]
        re = jnp.zeros((64, 256), F32)
        im = jnp.zeros((64, 256), F32)
        for i in range(boxes // 4):
            terms = lax.dot_general(
                lhs[512 * i : 512 * (i + 1), :], block, NT, preferred_element_type=F32
            )
            for j in range(4):
                b = 4 * i + j
                c = cosb[y, b : b + 1, :]
                d = sinb[y, b : b + 1, :]
                tre = terms[j * 128 : j * 128 + 64]
                tim = terms[j * 128 + 64 : (j + 1) * 128]
                re = re + (c * tre - d * tim)
                im = im + (d * tre + c * tim)
        pat = jnp.concatenate([re, im], axis=0).astype(BF16)
        pat = jnp.dot(perm, pat, preferred_element_type=F32)
        for h in range(2):
            send1[pl.ds((2 * y + h) * nbox, nbox)] = (
                pat[:, h * 128 : (h + 1) * 128].reshape(nbox, 8, 128).astype(BF16)
            )

        @pl.when(s == 0)
        def _():
            pl.semaphore_wait(barrier, total - 1)
            to_sibling.start()

        def send(g, j):
            pltpu.make_async_remote_copy(
                src_ref=send1.at[j * nbox + g],
                dst_ref=recv1.at[rank],
                send_sem=s1,
                recv_sem=r1,
                device_id=g * ndir + j,
                device_id_type=LOGICAL,
            ).start()

        for offset in far_groups(side)[:-1]:
            for h in range(2):
                send(group_at(offset), 2 * y + h)
        for h in range(2):
            j = 2 * y + h

            @pl.when(j != me)
            def _():
                send(box, j)

            @pl.when(j == me)
            def _():
                own1.start()

        return carry

    lax.fori_loop(0, chips, pattern_step, 0)

    to_other.start()

    def all_but_one(there, here, send_sem, recv_sem):
        return pltpu.make_async_remote_copy(
            src_ref=there.at[pl.ds(0, total - 1)],
            dst_ref=here.at[pl.ds(0, total - 1)],
            send_sem=send_sem,
            recv_sem=recv_sem,
            device_id=lax.rem(rank + 1, total),
            device_id_type=LOGICAL,
        )

    def near_box(x, own, b):
        count = ncount[b]
        gathered = jnp.concatenate(
            [
                x[jnp.where(k < count, nlist[k, b] - rank * boxes + own, boxes + half)]
                for k in range(8)
            ],
            axis=0,
        )
        zr = jnp.concatenate([zbuf[b, k, :, 0:128] for k in range(8)], axis=1)
        zi = jnp.concatenate([zbuf[b, k, :, 128:256] for k in range(8)], axis=1)
        both = jnp.dot(
            jnp.concatenate([zr, zi], axis=0), gathered, preferred_element_type=F32
        )
        cross = pltpu.roll(both[128:256], 64, 1)
        lane = lax.broadcasted_iota(jnp.int32, (128, 128), 1)
        near[b] = both[0:128] + jnp.where(lane < 64, -cross, cross)

    def near_sibling(i, carry):
        near_box(xsib, core * half, (1 - core) * half + i)
        return carry

    load_z.wait()
    for table in tables:
        table.wait()
    to_sibling.wait_recv()
    lax.fori_loop(0, half, near_sibling, 0)

    load_t.wait()
    own1.wait()
    all_but_one(send1, recv1, s1, r1).wait_recv()

    own2 = pltpu.make_async_copy(send2.at[rank], recv2.at[me * nbox + box], own_sem.at[1])
    sign = jnp.where(lax.broadcasted_iota(jnp.int32, (8, 128), 0) < 4, -1.0, 1.0)
    slots = src.shape[0]
    nothing = tr_hbm.shape[0]

    def group_of(s):
        code = sum(
            jnp.where(s == i, z * side + x, 0) for i, (z, x) in enumerate(far_groups(side))
        )
        return group_at((code // side, lax.rem(code, side)))

    def translate_group(s):
        g = group_of(s)
        for i in range(ndir):
            t = g * ndir + i
            straight = jnp.zeros((8, 128), F32)
            crossed = jnp.zeros((8, 128), F32)
            for k in range(slots):
                v = recv1[src[k, t]].astype(F32)
                tau = trans[jnp.where(k < used[t], off[k, t], nothing)]
                straight = straight + tau[0:1] * v
                crossed = crossed + tau[1:2] * v
            total_in = straight + sign * pltpu.roll(crossed, 4, 0)
            send2[t] = total_in.astype(BF16)

        for i in range(ndir):
            t = g * ndir + i

            @pl.when(t != rank)
            def _():
                pltpu.make_async_remote_copy(
                    src_ref=send2.at[t],
                    dst_ref=recv2.at[me * nbox + box],
                    send_sem=s2,
                    recv_sem=r2,
                    device_id=t,
                    device_id_type=LOGICAL,
                ).start()

            @pl.when(t == rank)
            def _():
                own2.start()


    def translate_step(s, carry):
        translate_group(s)
        return carry

    def mixed_step(i, carry):
        near_box(xoth, (1 - core) * half, core * half + i)
        translate_group(nbox // 2 + i)
        return carry

    lax.fori_loop(0, nbox // 2, translate_step, 0)
    to_other.wait_recv()
    lax.fori_loop(0, half, mixed_step, 0)

    own2.wait()
    all_but_one(send2, recv2, s2, r2).wait_recv()

    for y in range(chips):
        pair = jnp.concatenate(
            [
                recv2[(2 * y + h) * nbox : (2 * y + h + 1) * nbox]
                .astype(F32)
                .reshape(128, 128)
                .astype(BF16)
                for h in range(2)
            ],
            axis=1,
        )
        inc[:, y * 256 : (y + 1) * 256] = jnp.dot(perm_t, pair, preferred_element_type=F32)

    for i in range(boxes // 4):
        for j in range(4):
            b = 4 * i + j
            for y in range(chips):
                lanes = slice(y * 256, (y + 1) * 256)
                c = cosb[y, b : b + 1, :]
                d = sinb[y, b : b + 1, :]
                re = inc[0:64, lanes]
                im = inc[64:128, lanes]
                shf[i, j * 128 : j * 128 + 64, lanes] = (c * re + d * im).astype(BF16)
                shf[i, j * 128 + 64 : (j + 1) * 128, lanes] = (c * im - d * re).astype(BF16)
        mixed = jnp.dot(shf[i], a_ref[...], preferred_element_type=F32)
        for j in range(4):
            b = 4 * i + j
            m = mixed[j * 128 : (j + 1) * 128]
            far = jnp.concatenate(
                [m[0:64, 0:128] + m[64:128, 128:256], m[64:128, 0:128] - m[0:64, 128:256]], axis=0
            )
            out[b] = (near[b] + far.T).astype(BF16)

    to_sibling.wait_send()
    to_other.wait_send()
    all_but_one(send1, recv1, s1, r1).wait_send()
    all_but_one(send2, recv2, s2, r2).wait_send()


def local(
    nbox,
    ndir,
    currents,
    near_blocks,
    near_list,
    near_count,
    radiation,
    child_angle,
    translation,
    inter_src,
    inter_off,
    inter_count,
):
    boxes = currents.shape[0]
    total = nbox * ndir
    hbm = pl.BlockSpec(memory_space=pltpu.HBM)
    dma = pltpu.SemaphoreType.DMA
    return pl.pallas_call(
        functools.partial(kernel, nbox, ndir),
        out_shape=pltpu.VMEM((boxes, 128, 128), BF16),
        in_specs=[hbm] * 10,
        out_specs=pl.BlockSpec(memory_space=pltpu.VMEM),
        scratch_shapes=[
            pltpu.SMEM(near_list.shape[::-1], jnp.int32),
            pltpu.SMEM(near_count.shape, jnp.int32),
            pltpu.SMEM(inter_src.shape[::-1], jnp.int32),
            pltpu.SMEM(inter_off.shape[::-1], jnp.int32),
            pltpu.SMEM(inter_count.shape, jnp.int32),
            pltpu.VMEM((3 * boxes // 2 + 1, 128, 128), BF16),
            pltpu.VMEM((3 * boxes // 2 + 1, 128, 128), BF16),
            pltpu.VMEM(near_blocks.shape, BF16),
            pltpu.VMEM(radiation.shape, BF16),
            pltpu.VMEM(child_angle.shape, F32),
            pltpu.VMEM((translation.shape[0] + 4, 2, 128), F32),
            pltpu.VMEM((ndir // 2, boxes, 256), F32),
            pltpu.VMEM((ndir // 2, boxes, 256), F32),
            pltpu.VMEM((boxes * 128, 256), BF16),
            pltpu.VMEM((total, 8, 128), BF16),
            pltpu.VMEM((total, 8, 128), BF16),
            pltpu.VMEM((total, 8, 128), BF16),
            pltpu.VMEM((total, 8, 128), BF16),
            pltpu.VMEM((boxes, 128, 128), F32),
            pltpu.VMEM((128, ndir * 128), F32),
            pltpu.VMEM((boxes // 4, 512, ndir * 128), BF16),
            dma((6,)),
            dma((5,)),
            dma((2,)),
            dma,
            dma,
            dma,
            dma,
            dma((2,)),
            dma((2,)),
        ],
        compiler_params=pltpu.CompilerParams(
            collective_id=0, has_side_effects=True, vmem_limit_bytes=57 * 2**20
        ),
    )(
        near_list.T,
        near_count,
        inter_src.T,
        inter_off.T,
        inter_count,
        currents,
        near_blocks,
        radiation,
        child_angle,
        translation,
    )


def solution(mesh):
    nbox, ndir = mesh.shape["box"], mesh.shape["dir"]
    return jax.shard_map(
        functools.partial(local, nbox, ndir),
        mesh=mesh,
        in_specs=(
            P(("box", "dir"), None, None),
            P(("box", "dir"), None, None, None),
            P(("box", "dir"), None),
            P(("box", "dir")),
            P(),
            P(("box", "dir"), None),
            P(),
            P(),
            P(),
            P(),
        ),
        out_specs=P(("box", "dir"), None, None),
        check_vma=False,
    )
```

```python
import functools

import jax
import jax.numpy as jnp
from jax import lax
from jax.experimental import pallas as pl
from jax.experimental.pallas import tpu as pltpu
from jax.sharding import PartitionSpec as P

LOGICAL = pl.DeviceIdType.LOGICAL
F32 = jnp.float32
BF16 = jnp.bfloat16
NT = (((1,), (1,)), ((), ()))


def sincos(angle):
    h = angle * 0.5
    z = h * h
    s = -1.0 / 1307674368000.0
    for inv in (6227020800.0, -39916800.0, 362880.0, -5040.0, 120.0, -6.0, 1.0):
        s = s * z + 1.0 / inv
    s = s * h
    c = 1.0 / 20922789888000.0
    for inv in (-87178291200.0, 479001600.0, -3628800.0, 40320.0, -720.0, 24.0, -2.0, 1.0):
        c = c * z + 1.0 / inv
    return 2.0 * s * c, 1.0 - 2.0 * s * s


def far_groups(side):
    return sorted(
        ((z, x) for z in range(side) for x in range(side)),
        key=lambda o: -min(o[0], side - o[0]) - min(o[1], side - o[1]),
    )


def iota2(rows, columns):
    return (
        lax.broadcasted_iota(jnp.int32, (rows, columns), 0),
        lax.broadcasted_iota(jnp.int32, (rows, columns), 1),
    )


def kernel(
    nbox,
    ndir,
    list_hbm,
    count_hbm,
    src_hbm,
    off_hbm,
    used_hbm,
    x_hbm,
    z_hbm,
    a_hbm,
    ang_hbm,
    tr_hbm,
    out,
    nlist,
    ncount,
    src,
    off,
    used,
    xsib,
    xoth,
    zbuf,
    a_ref,
    ang,
    trans,
    cosb,
    sinb,
    lhs,
    send1,
    recv1,
    send2,
    recv2,
    near,
    inc,
    shf,
    load_sem,
    table_sem,
    own_sem,
    s1,
    r1,
    s2,
    r2,
    sh,
    rh,
):
    box = lax.axis_index("box")
    me = lax.axis_index("dir")
    chips = ndir // 2
    side = round(nbox**0.5)
    box_z, box_x = box // side, lax.rem(box, side)

    def group_at(offset):
        return lax.rem(box_z + offset[0], side) * side + lax.rem(box_x + offset[1], side)

    my_y = me // 2
    core = lax.rem(me, 2)
    boxes = x_hbm.shape[0]
    half = boxes // 2
    total = nbox * ndir
    rank = box * ndir + me

    barrier = pltpu.get_barrier_semaphore()
    for there in range(1, total):
        pl.semaphore_signal(
            barrier,
            inc=1,
            device_id=lax.rem(rank + there, total),
            device_id_type=LOGICAL,
        )

    load_x = pltpu.make_async_copy(x_hbm, xsib.at[pl.ds(core * half, boxes)], load_sem.at[0])
    load_o = pltpu.make_async_copy(x_hbm, xoth.at[pl.ds((1 - core) * half, boxes)], load_sem.at[5])
    load_a = pltpu.make_async_copy(a_hbm, a_ref, load_sem.at[1])
    load_g = pltpu.make_async_copy(ang_hbm, ang, load_sem.at[2])
    load_t = pltpu.make_async_copy(
        tr_hbm.at[:, :, pl.ds(pl.multiple_of(me * 128, 128), 128)],
        trans.at[pl.ds(0, tr_hbm.shape[0])],
        load_sem.at[3],
    )
    load_z = pltpu.make_async_copy(z_hbm, zbuf, load_sem.at[4])
    tables = [
        pltpu.make_async_copy(there, here, table_sem.at[i])
        for i, (there, here) in enumerate(
            (
                (list_hbm, nlist),
                (count_hbm, ncount),
                (src_hbm, src),
                (off_hbm, off),
                (used_hbm, used),
            )
        )
    ]
    load_g.start()
    load_x.start()
    load_a.start()
    load_o.start()
    load_t.start()
    for table in tables:
        table.start()
    load_z.start()

    xsib[boxes + half] = jnp.zeros((128, 128), BF16)
    xoth[boxes + half] = jnp.zeros((128, 128), BF16)
    trans[pl.ds(tr_hbm.shape[0], 4)] = jnp.zeros((4, 2, 128), F32)

    row, col = iota2(128, 128)
    within = lax.rem(row, 8)
    natural = 4 * lax.div(row, 8) + lax.rem(within, 4) + 64 * lax.div(within, 4)
    perm = jnp.where(col == natural, 1.0, 0.0).astype(BF16)
    within_t = lax.rem(col, 8)
    natural_t = 4 * lax.div(col, 8) + lax.rem(within_t, 4) + 64 * lax.div(within_t, 4)
    perm_t = jnp.where(row == natural_t, 1.0, 0.0).astype(BF16)
    row2, col2 = iota2(256, 128)
    spread = jnp.where(row2 == col2, 1.0, 0.0)
    spread = jnp.where((row2 >= 128) & (row2 < 192) & (col2 == row2 - 64), -1.0, spread)
    spread = jnp.where((row2 >= 192) & (col2 == row2 - 192), 1.0, spread).astype(BF16)

    load_g.wait()
    for y in range(chips):
        sn, cs = sincos(ang[:, y * 256 : (y + 1) * 256])
        sinb[y] = sn
        cosb[y] = cs

    load_x.wait()
    for i in range(boxes // 4):
        four = xsib[pl.ds(core * half + 4 * i, 4)].reshape(512, 128)
        turned = lax.dot_general(spread, four, NT, preferred_element_type=F32).astype(BF16)
        for j in range(4):
            rows = slice((4 * i + j) * 128, (4 * i + j + 1) * 128)
            lhs[rows, 0:128] = turned[0:128, j * 128 : (j + 1) * 128]
            lhs[rows, 128:256] = turned[128:256, j * 128 : (j + 1) * 128]

    load_a.wait()
    load_o.wait()

    own1 = pltpu.make_async_copy(send1.at[me * nbox + box], recv1.at[rank], own_sem.at[0])

    to_sibling = pltpu.make_async_remote_copy(
        src_ref=xsib.at[pl.ds(half, half)],
        dst_ref=xsib.at[pl.ds(core * boxes, half)],
        send_sem=sh.at[0],
        recv_sem=rh.at[0],
        device_id=rank + 1 - 2 * core,
        device_id_type=LOGICAL,
    )
    to_other = pltpu.make_async_remote_copy(
        src_ref=xoth.at[pl.ds(half, half)],
        dst_ref=xoth.at[pl.ds((1 - core) * boxes, half)],
        send_sem=sh.at[1],
        recv_sem=rh.at[1],
        device_id=lax.rem(rank + total - 1 + 2 * core, total),
        device_id_type=LOGICAL,
    )

    def pattern_step(s, carry):
        y = lax.rem(my_y + jnp.where(s == 0, 2, jnp.where(s == 1, 1, jnp.where(s == 2, 3, 0))), chips)
        block = a_ref[pl.ds(pl.multiple_of(y * 256, 256), 256), :]
        re = jnp.zeros((64, 256), F32)
        im = jnp.zeros((64, 256), F32)
        for i in range(boxes // 4):
            terms = lax.dot_general(
                lhs[512 * i : 512 * (i + 1), :], block, NT, preferred_element_type=F32
            )
            for j in range(4):
                b = 4 * i + j
                c = cosb[y, b : b + 1, :]
                d = sinb[y, b : b + 1, :]
                tre = terms[j * 128 : j * 128 + 64]
                tim = terms[j * 128 + 64 : (j + 1) * 128]
                re = re + (c * tre - d * tim)
                im = im + (d * tre + c * tim)
        pat = jnp.concatenate([re, im], axis=0).astype(BF16)
        pat = jnp.dot(perm, pat, preferred_element_type=F32)
        for h in range(2):
            send1[pl.ds((2 * y + h) * nbox, nbox)] = (
                pat[:, h * 128 : (h + 1) * 128].reshape(nbox, 8, 128).astype(BF16)
            )

        @pl.when(s == 0)
        def _():
            pl.semaphore_wait(barrier, total - 1)
            to_sibling.start()

        def send(g, j):
            pltpu.make_async_remote_copy(
                src_ref=send1.at[j * nbox + g],
                dst_ref=recv1.at[rank],
                send_sem=s1,
                recv_sem=r1,
                device_id=g * ndir + j,
                device_id_type=LOGICAL,
            ).start()

        for offset in far_groups(side)[:-1]:
            for h in range(2):
                send(group_at(offset), 2 * y + h)
        for h in range(2):
            j = 2 * y + h

            @pl.when(j != me)
            def _():
                send(box, j)

            @pl.when(j == me)
            def _():
                own1.start()

        return carry

    lax.fori_loop(0, chips, pattern_step, 0)

    to_other.start()

    def all_but_one(there, here, send_sem, recv_sem):
        return pltpu.make_async_remote_copy(
            src_ref=there.at[pl.ds(0, total - 1)],
            dst_ref=here.at[pl.ds(0, total - 1)],
            send_sem=send_sem,
            recv_sem=recv_sem,
            device_id=lax.rem(rank + 1, total),
            device_id_type=LOGICAL,
        )

    def near_box(x, own, b):
        count = ncount[b]
        gathered = jnp.concatenate(
            [
                x[jnp.where(k < count, nlist[k, b] - rank * boxes + own, boxes + half)]
                for k in range(8)
            ],
            axis=0,
        )
        zr = jnp.concatenate([zbuf[b, k, :, 0:128] for k in range(8)], axis=1)
        zi = jnp.concatenate([zbuf[b, k, :, 128:256] for k in range(8)], axis=1)
        both = jnp.dot(
            jnp.concatenate([zr, zi], axis=0), gathered, preferred_element_type=F32
        )
        cross = pltpu.roll(both[128:256], 64, 1)
        lane = lax.broadcasted_iota(jnp.int32, (128, 128), 1)
        near[b] = both[0:128] + jnp.where(lane < 64, -cross, cross)

    def near_sibling(i, carry):
        near_box(xsib, core * half, (1 - core) * half + i)
        return carry

    load_z.wait()
    for table in tables:
        table.wait()
    to_sibling.wait_recv()
    lax.fori_loop(0, half, near_sibling, 0)

    load_t.wait()
    own1.wait()
    all_but_one(send1, recv1, s1, r1).wait_recv()

    own2 = pltpu.make_async_copy(send2.at[rank], recv2.at[me * nbox + box], own_sem.at[1])
    sign = jnp.where(lax.broadcasted_iota(jnp.int32, (8, 128), 0) < 4, -1.0, 1.0)
    slots = src.shape[0]
    nothing = tr_hbm.shape[0]

    def group_of(s):
        code = sum(
            jnp.where(s == i, z * side + x, 0) for i, (z, x) in enumerate(far_groups(side))
        )
        return group_at((code // side, lax.rem(code, side)))

    def translate_group(s):
        g = group_of(s)
        for i in range(ndir):
            t = g * ndir + i
            straight = jnp.zeros((8, 128), F32)
            crossed = jnp.zeros((8, 128), F32)
            for k in range(slots):
                v = recv1[src[k, t]].astype(F32)
                tau = trans[jnp.where(k < used[t], off[k, t], nothing)]
                straight = straight + tau[0:1] * v
                crossed = crossed + tau[1:2] * v
            total_in = straight + sign * pltpu.roll(crossed, 4, 0)
            send2[t] = total_in.astype(BF16)

        for i in range(ndir):
            t = g * ndir + i

            @pl.when(t != rank)
            def _():
                pltpu.make_async_remote_copy(
                    src_ref=send2.at[t],
                    dst_ref=recv2.at[me * nbox + box],
                    send_sem=s2,
                    recv_sem=r2,
                    device_id=t,
                    device_id_type=LOGICAL,
                ).start()

            @pl.when(t == rank)
            def _():
                own2.start()


    def translate_step(s, carry):
        translate_group(s)
        return carry

    def near_other(i, carry):
        near_box(xoth, (1 - core) * half, core * half + i)
        return carry

    lax.fori_loop(0, nbox, translate_step, 0)
    to_other.wait_recv()
    lax.fori_loop(0, half, near_other, 0)

    own2.wait()
    all_but_one(send2, recv2, s2, r2).wait_recv()

    for y in range(chips):
        pair = jnp.concatenate(
            [
                recv2[(2 * y + h) * nbox : (2 * y + h + 1) * nbox]
                .astype(F32)
                .reshape(128, 128)
                .astype(BF16)
                for h in range(2)
            ],
            axis=1,
        )
        inc[:, y * 256 : (y + 1) * 256] = jnp.dot(perm_t, pair, preferred_element_type=F32)

    for i in range(boxes // 4):
        for j in range(4):
            b = 4 * i + j
            for y in range(chips):
                lanes = slice(y * 256, (y + 1) * 256)
                c = cosb[y, b : b + 1, :]
                d = sinb[y, b : b + 1, :]
                re = inc[0:64, lanes]
                im = inc[64:128, lanes]
                shf[i, j * 128 : j * 128 + 64, lanes] = (c * re + d * im).astype(BF16)
                shf[i, j * 128 + 64 : (j + 1) * 128, lanes] = (c * im - d * re).astype(BF16)
        mixed = jnp.dot(shf[i], a_ref[...], preferred_element_type=F32)
        for j in range(4):
            b = 4 * i + j
            m = mixed[j * 128 : (j + 1) * 128]
            far = jnp.concatenate(
                [m[0:64, 0:128] + m[64:128, 128:256], m[64:128, 0:128] - m[0:64, 128:256]], axis=0
            )
            out[b] = (near[b] + far.T).astype(BF16)

    to_sibling.wait_send()
    to_other.wait_send()
    all_but_one(send1, recv1, s1, r1).wait_send()
    all_but_one(send2, recv2, s2, r2).wait_send()


def local(
    nbox,
    ndir,
    currents,
    near_blocks,
    near_list,
    near_count,
    radiation,
    child_angle,
    translation,
    inter_src,
    inter_off,
    inter_count,
):
    boxes = currents.shape[0]
    total = nbox * ndir
    hbm = pl.BlockSpec(memory_space=pltpu.HBM)
    dma = pltpu.SemaphoreType.DMA
    return pl.pallas_call(
        functools.partial(kernel, nbox, ndir),
        out_shape=pltpu.VMEM((boxes, 128, 128), BF16),
        in_specs=[hbm] * 10,
        out_specs=pl.BlockSpec(memory_space=pltpu.VMEM),
        scratch_shapes=[
            pltpu.SMEM(near_list.shape[::-1], jnp.int32),
            pltpu.SMEM(near_count.shape, jnp.int32),
            pltpu.SMEM(inter_src.shape[::-1], jnp.int32),
            pltpu.SMEM(inter_off.shape[::-1], jnp.int32),
            pltpu.SMEM(inter_count.shape, jnp.int32),
            pltpu.VMEM((3 * boxes // 2 + 1, 128, 128), BF16),
            pltpu.VMEM((3 * boxes // 2 + 1, 128, 128), BF16),
            pltpu.VMEM(near_blocks.shape, BF16),
            pltpu.VMEM(radiation.shape, BF16),
            pltpu.VMEM(child_angle.shape, F32),
            pltpu.VMEM((translation.shape[0] + 4, 2, 128), F32),
            pltpu.VMEM((ndir // 2, boxes, 256), F32),
            pltpu.VMEM((ndir // 2, boxes, 256), F32),
            pltpu.VMEM((boxes * 128, 256), BF16),
            pltpu.VMEM((total, 8, 128), BF16),
            pltpu.VMEM((total, 8, 128), BF16),
            pltpu.VMEM((total, 8, 128), BF16),
            pltpu.VMEM((total, 8, 128), BF16),
            pltpu.VMEM((boxes, 128, 128), F32),
            pltpu.VMEM((128, ndir * 128), F32),
            pltpu.VMEM((boxes // 4, 512, ndir * 128), BF16),
            dma((6,)),
            dma((5,)),
            dma((2,)),
            dma,
            dma,
            dma,
            dma,
            dma((2,)),
            dma((2,)),
        ],
        compiler_params=pltpu.CompilerParams(
            collective_id=0, has_side_effects=True, vmem_limit_bytes=57 * 2**20
        ),
    )(
        near_list.T,
        near_count,
        inter_src.T,
        inter_off.T,
        inter_count,
        currents,
        near_blocks,
        radiation,
        child_angle,
        translation,
    )


def solution(mesh):
    nbox, ndir = mesh.shape["box"], mesh.shape["dir"]
    return jax.shard_map(
        functools.partial(local, nbox, ndir),
        mesh=mesh,
        in_specs=(
            P(("box", "dir"), None, None),
            P(("box", "dir"), None, None, None),
            P(("box", "dir"), None),
            P(("box", "dir")),
            P(),
            P(("box", "dir"), None),
            P(),
            P(),
            P(),
            P(),
        ),
        out_specs=P(("box", "dir"), None, None),
        check_vma=False,
    )
```

```python
import functools

import jax
import jax.numpy as jnp
from jax import lax
from jax.experimental import pallas as pl
from jax.experimental.pallas import tpu as pltpu
from jax.sharding import PartitionSpec as P

LOGICAL = pl.DeviceIdType.LOGICAL
F32 = jnp.float32
BF16 = jnp.bfloat16
NT = (((1,), (1,)), ((), ()))


def sincos(angle):
    h = angle * 0.5
    z = h * h
    s = -1.0 / 1307674368000.0
    for inv in (6227020800.0, -39916800.0, 362880.0, -5040.0, 120.0, -6.0, 1.0):
        s = s * z + 1.0 / inv
    s = s * h
    c = 1.0 / 20922789888000.0
    for inv in (-87178291200.0, 479001600.0, -3628800.0, 40320.0, -720.0, 24.0, -2.0, 1.0):
        c = c * z + 1.0 / inv
    return 2.0 * s * c, 1.0 - 2.0 * s * s


def far_groups(side):
    return sorted(
        ((z, x) for z in range(side) for x in range(side)),
        key=lambda o: -min(o[0], side - o[0]) - min(o[1], side - o[1]),
    )


def iota2(rows, columns):
    return (
        lax.broadcasted_iota(jnp.int32, (rows, columns), 0),
        lax.broadcasted_iota(jnp.int32, (rows, columns), 1),
    )


def kernel(
    nbox,
    ndir,
    list_hbm,
    count_hbm,
    src_hbm,
    off_hbm,
    used_hbm,
    x_hbm,
    z_hbm,
    a_hbm,
    ang_hbm,
    tr_hbm,
    out,
    nlist,
    ncount,
    src,
    off,
    used,
    op,
    xsib,
    xoth,
    zbuf,
    a_ref,
    ang,
    trans,
    cosb,
    sinb,
    lhs,
    send1,
    recv1,
    send2,
    recv2,
    near,
    inc,
    shf,
    load_sem,
    table_sem,
    own_sem,
    s1,
    r1,
    s2,
    r2,
    sh,
    rh,
):
    box = lax.axis_index("box")
    me = lax.axis_index("dir")
    chips = ndir // 2
    side = round(nbox**0.5)
    box_z, box_x = box // side, lax.rem(box, side)

    def group_at(offset):
        return lax.rem(box_z + offset[0], side) * side + lax.rem(box_x + offset[1], side)

    my_y = me // 2
    core = lax.rem(me, 2)
    boxes = x_hbm.shape[0]
    half = boxes // 2
    total = nbox * ndir
    rank = box * ndir + me

    barrier = pltpu.get_barrier_semaphore()
    groups = [group_at(offset) for offset in far_groups(side)]
    peers = [lax.rem(me + 2 * k + c, ndir) for k in (2, 1, 3, 0) for c in range(2)]
    for d in peers:
        for g in groups:
            if d is not peers[-2] or g is not groups[-1]:
                pl.semaphore_signal(
                    barrier, inc=1, device_id=g * ndir + d, device_id_type=LOGICAL
                )

    load_x = pltpu.make_async_copy(x_hbm, xsib.at[pl.ds(core * half, boxes)], load_sem.at[0])
    load_o = pltpu.make_async_copy(x_hbm, xoth.at[pl.ds((1 - core) * half, boxes)], load_sem.at[5])
    load_a = pltpu.make_async_copy(a_hbm, a_ref, load_sem.at[1])
    load_g = pltpu.make_async_copy(ang_hbm, ang, load_sem.at[2])
    load_t = pltpu.make_async_copy(
        tr_hbm.at[:, :, pl.ds(pl.multiple_of(me * 128, 128), 128)],
        trans.at[pl.ds(0, tr_hbm.shape[0])],
        load_sem.at[3],
    )
    load_z = pltpu.make_async_copy(z_hbm, zbuf, load_sem.at[4])
    tables = [
        pltpu.make_async_copy(there, here, table_sem.at[i])
        for i, (there, here) in enumerate(
            (
                (list_hbm, nlist),
                (count_hbm, ncount),
                (src_hbm, src),
                (off_hbm, off),
                (used_hbm, used),
            )
        )
    ]
    load_g.start()
    load_x.start()
    load_a.start()
    load_o.start()
    load_t.start()
    for table in tables:
        table.start()
    load_z.start()

    xsib[boxes + half] = jnp.zeros((128, 128), BF16)
    xoth[boxes + half] = jnp.zeros((128, 128), BF16)
    trans[pl.ds(tr_hbm.shape[0], 4)] = jnp.zeros((4, 2, 128), F32)

    row, col = iota2(128, 128)
    within = lax.rem(row, 8)
    natural = 4 * lax.div(row, 8) + lax.rem(within, 4) + 64 * lax.div(within, 4)
    perm = jnp.where(col == natural, 1.0, 0.0).astype(BF16)
    within_t = lax.rem(col, 8)
    natural_t = 4 * lax.div(col, 8) + lax.rem(within_t, 4) + 64 * lax.div(within_t, 4)
    perm_t = jnp.where(row == natural_t, 1.0, 0.0).astype(BF16)
    row2, col2 = iota2(256, 128)
    spread = jnp.where(row2 == col2, 1.0, 0.0)
    spread = jnp.where((row2 >= 128) & (row2 < 192) & (col2 == row2 - 64), -1.0, spread)
    spread = jnp.where((row2 >= 192) & (col2 == row2 - 192), 1.0, spread).astype(BF16)

    load_g.wait()
    for y in range(chips):
        sn, cs = sincos(ang[:, y * 256 : (y + 1) * 256])
        sinb[y] = sn
        cosb[y] = cs

    load_x.wait()
    for i in range(boxes // 4):
        four = xsib[pl.ds(core * half + 4 * i, 4)].reshape(512, 128)
        turned = lax.dot_general(spread, four, NT, preferred_element_type=F32).astype(BF16)
        for j in range(4):
            rows = slice((4 * i + j) * 128, (4 * i + j + 1) * 128)
            lhs[rows, 0:128] = turned[0:128, j * 128 : (j + 1) * 128]
            lhs[rows, 128:256] = turned[128:256, j * 128 : (j + 1) * 128]

    load_a.wait()
    load_o.wait()

    own1 = pltpu.make_async_copy(send1.at[me * nbox + box], recv1.at[rank], own_sem.at[0])

    to_sibling = pltpu.make_async_remote_copy(
        src_ref=xsib.at[pl.ds(half, half)],
        dst_ref=xsib.at[pl.ds(core * boxes, half)],
        send_sem=sh.at[0],
        recv_sem=rh.at[0],
        device_id=rank + 1 - 2 * core,
        device_id_type=LOGICAL,
    )
    to_other = pltpu.make_async_remote_copy(
        src_ref=xoth.at[pl.ds(half, half)],
        dst_ref=xoth.at[pl.ds((1 - core) * boxes, half)],
        send_sem=sh.at[1],
        recv_sem=rh.at[1],
        device_id=lax.rem(rank + total - 1 + 2 * core, total),
        device_id_type=LOGICAL,
    )

    def pattern_step(s, carry):
        y = lax.rem(my_y + jnp.where(s == 0, 2, jnp.where(s == 1, 1, jnp.where(s == 2, 3, 0))), chips)
        block = a_ref[pl.ds(pl.multiple_of(y * 256, 256), 256), :]
        re = jnp.zeros((64, 256), F32)
        im = jnp.zeros((64, 256), F32)
        for i in range(boxes // 4):
            terms = lax.dot_general(
                lhs[512 * i : 512 * (i + 1), :], block, NT, preferred_element_type=F32
            )
            for j in range(4):
                b = 4 * i + j
                c = cosb[y, b : b + 1, :]
                d = sinb[y, b : b + 1, :]
                tre = terms[j * 128 : j * 128 + 64]
                tim = terms[j * 128 + 64 : (j + 1) * 128]
                re = re + (c * tre - d * tim)
                im = im + (d * tre + c * tim)
        pat = jnp.concatenate([re, im], axis=0).astype(BF16)
        pat = jnp.dot(perm, pat, preferred_element_type=F32)
        for h in range(2):
            send1[pl.ds((2 * y + h) * nbox, nbox)] = (
                pat[:, h * 128 : (h + 1) * 128].reshape(nbox, 8, 128).astype(BF16)
            )

        @pl.when(s == 0)
        def _():
            pl.semaphore_wait(barrier, total - 1)
            to_sibling.start()

        def send(g, j):
            pltpu.make_async_remote_copy(
                src_ref=send1.at[j * nbox + g],
                dst_ref=recv1.at[rank],
                send_sem=s1,
                recv_sem=r1,
                device_id=g * ndir + j,
                device_id_type=LOGICAL,
            ).start()

        for g in groups[:-1]:
            for h in range(2):
                send(g, 2 * y + h)
        for h in range(2):
            j = 2 * y + h

            @pl.when(j != me)
            def _():
                send(box, j)

            @pl.when(j == me)
            def _():
                own1.start()

        return carry

    lax.fori_loop(0, chips, pattern_step, 0)

    to_other.start()

    def all_but_one(there, here, send_sem, recv_sem):
        return pltpu.make_async_remote_copy(
            src_ref=there.at[pl.ds(0, total - 1)],
            dst_ref=here.at[pl.ds(0, total - 1)],
            send_sem=send_sem,
            recv_sem=recv_sem,
            device_id=lax.rem(rank + 1, total),
            device_id_type=LOGICAL,
        )

    def near_box(x, own, b):
        count = ncount[b]
        gathered = jnp.concatenate(
            [
                x[jnp.where(k < count, nlist[k, b] - rank * boxes + own, boxes + half)]
                for k in range(8)
            ],
            axis=0,
        )
        zr = jnp.concatenate([zbuf[b, k, :, 0:128] for k in range(8)], axis=1)
        zi = jnp.concatenate([zbuf[b, k, :, 128:256] for k in range(8)], axis=1)
        both = jnp.dot(
            jnp.concatenate([zr, zi], axis=0), gathered, preferred_element_type=F32
        )
        cross = pltpu.roll(both[128:256], 64, 1)
        lane = lax.broadcasted_iota(jnp.int32, (128, 128), 1)
        near[b] = both[0:128] + jnp.where(lane < 64, -cross, cross)

    def near_sibling(i, carry):
        near_box(xsib, core * half, (1 - core) * half + i)
        return carry

    for table in tables:
        table.wait()
    slots = src.shape[0]
    nothing = tr_hbm.shape[0]

    def live_step(t, carry):
        for k in range(slots):
            op[k, t] = jnp.where(k < used[t], off[k, t], nothing)
        return carry

    lax.fori_loop(0, total, live_step, 0, unroll=4)
    load_z.wait()
    to_sibling.wait_recv()
    lax.fori_loop(0, half, near_sibling, 0)

    load_t.wait()
    own1.wait()
    all_but_one(send1, recv1, s1, r1).wait_recv()

    own2 = pltpu.make_async_copy(send2.at[rank], recv2.at[me * nbox + box], own_sem.at[1])
    sign = jnp.where(lax.broadcasted_iota(jnp.int32, (8, 128), 0) < 4, -1.0, 1.0)

    def group_of(s):
        code = sum(
            jnp.where(s == i, z * side + x, 0) for i, (z, x) in enumerate(far_groups(side))
        )
        return group_at((code // side, lax.rem(code, side)))

    def translate_group(s):
        g = group_of(s)
        for i in range(ndir):
            t = g * ndir + i
            straight = jnp.zeros((8, 128), F32)
            crossed = jnp.zeros((8, 128), F32)
            for k in range(slots):
                v = recv1[src[k, t]].astype(F32)
                tau = trans[op[k, t]]
                straight = straight + tau[0:1] * v
                crossed = crossed + tau[1:2] * v
            total_in = straight + sign * pltpu.roll(crossed, 4, 0)
            send2[t] = total_in.astype(BF16)

        for i in range(ndir):
            t = g * ndir + i

            @pl.when(t != rank)
            def _():
                pltpu.make_async_remote_copy(
                    src_ref=send2.at[t],
                    dst_ref=recv2.at[me * nbox + box],
                    send_sem=s2,
                    recv_sem=r2,
                    device_id=t,
                    device_id_type=LOGICAL,
                ).start()

            @pl.when(t == rank)
            def _():
                own2.start()


    def translate_step(s, carry):
        translate_group(s)
        return carry

    def near_other(i, carry):
        near_box(xoth, (1 - core) * half, core * half + i)
        return carry

    lax.fori_loop(0, nbox, translate_step, 0)
    to_other.wait_recv()
    lax.fori_loop(0, half, near_other, 0)

    own2.wait()
    all_but_one(send2, recv2, s2, r2).wait_recv()

    for y in range(chips):
        pair = jnp.concatenate(
            [
                recv2[(2 * y + h) * nbox : (2 * y + h + 1) * nbox]
                .astype(F32)
                .reshape(128, 128)
                .astype(BF16)
                for h in range(2)
            ],
            axis=1,
        )
        inc[:, y * 256 : (y + 1) * 256] = jnp.dot(perm_t, pair, preferred_element_type=F32)

    for i in range(boxes // 4):
        for j in range(4):
            b = 4 * i + j
            for y in range(chips):
                lanes = slice(y * 256, (y + 1) * 256)
                c = cosb[y, b : b + 1, :]
                d = sinb[y, b : b + 1, :]
                re = inc[0:64, lanes]
                im = inc[64:128, lanes]
                shf[i, j * 128 : j * 128 + 64, lanes] = (c * re + d * im).astype(BF16)
                shf[i, j * 128 + 64 : (j + 1) * 128, lanes] = (c * im - d * re).astype(BF16)
        mixed = jnp.dot(shf[i], a_ref[...], preferred_element_type=F32)
        for j in range(4):
            b = 4 * i + j
            m = mixed[j * 128 : (j + 1) * 128]
            far = jnp.concatenate(
                [m[0:64, 0:128] + m[64:128, 128:256], m[64:128, 0:128] - m[0:64, 128:256]], axis=0
            )
            out[b] = (near[b] + far.T).astype(BF16)

    to_sibling.wait_send()
    to_other.wait_send()
    all_but_one(send1, recv1, s1, r1).wait_send()
    all_but_one(send2, recv2, s2, r2).wait_send()


def local(
    nbox,
    ndir,
    currents,
    near_blocks,
    near_list,
    near_count,
    radiation,
    child_angle,
    translation,
    inter_src,
    inter_off,
    inter_count,
):
    boxes = currents.shape[0]
    total = nbox * ndir
    hbm = pl.BlockSpec(memory_space=pltpu.HBM)
    dma = pltpu.SemaphoreType.DMA
    return pl.pallas_call(
        functools.partial(kernel, nbox, ndir),
        out_shape=pltpu.VMEM((boxes, 128, 128), BF16),
        in_specs=[hbm] * 10,
        out_specs=pl.BlockSpec(memory_space=pltpu.VMEM),
        scratch_shapes=[
            pltpu.SMEM(near_list.shape[::-1], jnp.int32),
            pltpu.SMEM(near_count.shape, jnp.int32),
            pltpu.SMEM(inter_src.shape[::-1], jnp.int32),
            pltpu.SMEM(inter_off.shape[::-1], jnp.int32),
            pltpu.SMEM(inter_count.shape, jnp.int32),
            pltpu.SMEM(inter_off.shape[::-1], jnp.int32),
            pltpu.VMEM((3 * boxes // 2 + 1, 128, 128), BF16),
            pltpu.VMEM((3 * boxes // 2 + 1, 128, 128), BF16),
            pltpu.VMEM(near_blocks.shape, BF16),
            pltpu.VMEM(radiation.shape, BF16),
            pltpu.VMEM(child_angle.shape, F32),
            pltpu.VMEM((translation.shape[0] + 4, 2, 128), F32),
            pltpu.VMEM((ndir // 2, boxes, 256), F32),
            pltpu.VMEM((ndir // 2, boxes, 256), F32),
            pltpu.VMEM((boxes * 128, 256), BF16),
            pltpu.VMEM((total, 8, 128), BF16),
            pltpu.VMEM((total, 8, 128), BF16),
            pltpu.VMEM((total, 8, 128), BF16),
            pltpu.VMEM((total, 8, 128), BF16),
            pltpu.VMEM((boxes, 128, 128), F32),
            pltpu.VMEM((128, ndir * 128), F32),
            pltpu.VMEM((boxes // 4, 512, ndir * 128), BF16),
            dma((6,)),
            dma((5,)),
            dma((2,)),
            dma,
            dma,
            dma,
            dma,
            dma((2,)),
            dma((2,)),
        ],
        compiler_params=pltpu.CompilerParams(
            collective_id=0, has_side_effects=True, vmem_limit_bytes=57 * 2**20
        ),
    )(
        near_list.T,
        near_count,
        inter_src.T,
        inter_off.T,
        inter_count,
        currents,
        near_blocks,
        radiation,
        child_angle,
        translation,
    )


def solution(mesh):
    nbox, ndir = mesh.shape["box"], mesh.shape["dir"]
    return jax.shard_map(
        functools.partial(local, nbox, ndir),
        mesh=mesh,
        in_specs=(
            P(("box", "dir"), None, None),
            P(("box", "dir"), None, None, None),
            P(("box", "dir"), None),
            P(("box", "dir")),
            P(),
            P(("box", "dir"), None),
            P(),
            P(),
            P(),
            P(),
        ),
        out_specs=P(("box", "dir"), None, None),
        check_vma=False,
    )
```

```python
import functools

import jax
import jax.numpy as jnp
from jax import lax
from jax.experimental import pallas as pl
from jax.experimental.pallas import tpu as pltpu
from jax.sharding import PartitionSpec as P

LOGICAL = pl.DeviceIdType.LOGICAL
F32 = jnp.float32
BF16 = jnp.bfloat16
NT = (((1,), (1,)), ((), ()))


def sincos(angle):
    h = angle * 0.5
    z = h * h
    s = -1.0 / 1307674368000.0
    for inv in (6227020800.0, -39916800.0, 362880.0, -5040.0, 120.0, -6.0, 1.0):
        s = s * z + 1.0 / inv
    s = s * h
    c = 1.0 / 20922789888000.0
    for inv in (-87178291200.0, 479001600.0, -3628800.0, 40320.0, -720.0, 24.0, -2.0, 1.0):
        c = c * z + 1.0 / inv
    return 2.0 * s * c, 1.0 - 2.0 * s * s


def far_groups(side):
    return sorted(
        ((z, x) for z in range(side) for x in range(side)),
        key=lambda o: -min(o[0], side - o[0]) - min(o[1], side - o[1]),
    )


def iota2(rows, columns):
    return (
        lax.broadcasted_iota(jnp.int32, (rows, columns), 0),
        lax.broadcasted_iota(jnp.int32, (rows, columns), 1),
    )


def kernel(
    nbox,
    ndir,
    list_hbm,
    count_hbm,
    src_hbm,
    off_hbm,
    used_hbm,
    x_hbm,
    z_hbm,
    a_hbm,
    ang_hbm,
    tr_hbm,
    out,
    nlist,
    ncount,
    src,
    off,
    used,
    op,
    xsib,
    xoth,
    zbuf,
    a_ref,
    ang,
    trans,
    cosb,
    sinb,
    lhs,
    send1,
    recv1,
    send2,
    recv2,
    near,
    inc,
    shf,
    load_sem,
    table_sem,
    own_sem,
    s1,
    r1,
    s2,
    r2,
    sh,
    rh,
):
    box = lax.axis_index("box")
    me = lax.axis_index("dir")
    chips = ndir // 2
    side = round(nbox**0.5)
    box_z, box_x = box // side, lax.rem(box, side)

    def group_at(offset):
        return lax.rem(box_z + offset[0], side) * side + lax.rem(box_x + offset[1], side)

    my_y = me // 2
    core = lax.rem(me, 2)
    boxes = x_hbm.shape[0]
    half = boxes // 2
    total = nbox * ndir
    rank = box * ndir + me

    barrier = pltpu.get_barrier_semaphore()
    groups = [group_at(offset) for offset in far_groups(side)]
    peers = [lax.rem(me + 2 * k + c, ndir) for k in (2, 1, 3, 0) for c in range(2)]
    for d in peers:
        for g in groups:
            if d is not peers[-2] or g is not groups[-1]:
                pl.semaphore_signal(
                    barrier, inc=1, device_id=g * ndir + d, device_id_type=LOGICAL
                )

    load_x = pltpu.make_async_copy(x_hbm, xsib.at[pl.ds(core * half, boxes)], load_sem.at[0])
    load_o = pltpu.make_async_copy(x_hbm, xoth.at[pl.ds((1 - core) * half, boxes)], load_sem.at[5])
    load_a = pltpu.make_async_copy(a_hbm, a_ref, load_sem.at[1])
    load_g = pltpu.make_async_copy(ang_hbm, ang, load_sem.at[2])
    load_t = pltpu.make_async_copy(
        tr_hbm.at[:, :, pl.ds(pl.multiple_of(me * 128, 128), 128)],
        trans.at[pl.ds(0, tr_hbm.shape[0])],
        load_sem.at[3],
    )
    load_z = pltpu.make_async_copy(z_hbm, zbuf, load_sem.at[4])
    tables = [
        pltpu.make_async_copy(there, here, table_sem.at[i])
        for i, (there, here) in enumerate(
            (
                (list_hbm, nlist),
                (count_hbm, ncount),
                (src_hbm, src),
                (off_hbm, off),
                (used_hbm, used),
            )
        )
    ]
    load_g.start()
    load_x.start()
    load_a.start()
    load_o.start()
    load_t.start()
    for table in tables:
        table.start()
    load_z.start()

    xsib[boxes + half] = jnp.zeros((128, 128), BF16)
    xoth[boxes + half] = jnp.zeros((128, 128), BF16)
    trans[pl.ds(tr_hbm.shape[0], 4)] = jnp.zeros((4, 2, 128), F32)

    row, col = iota2(128, 128)
    within = lax.rem(row, 8)
    natural = 4 * lax.div(row, 8) + lax.rem(within, 4) + 64 * lax.div(within, 4)
    perm = jnp.where(col == natural, 1.0, 0.0).astype(BF16)
    within_t = lax.rem(col, 8)
    natural_t = 4 * lax.div(col, 8) + lax.rem(within_t, 4) + 64 * lax.div(within_t, 4)
    perm_t = jnp.where(row == natural_t, 1.0, 0.0).astype(BF16)
    row2, col2 = iota2(256, 128)
    spread = jnp.where(row2 == col2, 1.0, 0.0)
    spread = jnp.where((row2 >= 128) & (row2 < 192) & (col2 == row2 - 64), -1.0, spread)
    spread = jnp.where((row2 >= 192) & (col2 == row2 - 192), 1.0, spread).astype(BF16)

    load_g.wait()
    for y in range(chips):
        sn, cs = sincos(ang[:, y * 256 : (y + 1) * 256])
        sinb[y] = sn
        cosb[y] = cs

    load_x.wait()
    for i in range(boxes // 4):
        four = xsib[pl.ds(core * half + 4 * i, 4)].reshape(512, 128)
        turned = lax.dot_general(spread, four, NT, preferred_element_type=F32).astype(BF16)
        for j in range(4):
            rows = slice((4 * i + j) * 128, (4 * i + j + 1) * 128)
            lhs[rows, 0:128] = turned[0:128, j * 128 : (j + 1) * 128]
            lhs[rows, 128:256] = turned[128:256, j * 128 : (j + 1) * 128]

    load_a.wait()
    load_o.wait()

    own1 = pltpu.make_async_copy(send1.at[me * nbox + box], recv1.at[rank], own_sem.at[0])

    to_sibling = pltpu.make_async_remote_copy(
        src_ref=xsib.at[pl.ds(half, half)],
        dst_ref=xsib.at[pl.ds(core * boxes, half)],
        send_sem=sh.at[0],
        recv_sem=rh.at[0],
        device_id=rank + 1 - 2 * core,
        device_id_type=LOGICAL,
    )
    to_other = pltpu.make_async_remote_copy(
        src_ref=xoth.at[pl.ds(half, half)],
        dst_ref=xoth.at[pl.ds((1 - core) * boxes, half)],
        send_sem=sh.at[1],
        recv_sem=rh.at[1],
        device_id=lax.rem(rank + total - 1 + 2 * core, total),
        device_id_type=LOGICAL,
    )

    def pattern_step(s, carry):
        y = lax.rem(my_y + jnp.where(s == 0, 2, jnp.where(s == 1, 1, jnp.where(s == 2, 3, 0))), chips)
        block = a_ref[pl.ds(pl.multiple_of(y * 256, 256), 256), :]
        re = jnp.zeros((64, 256), F32)
        im = jnp.zeros((64, 256), F32)
        for i in range(boxes // 4):
            terms = lax.dot_general(
                lhs[512 * i : 512 * (i + 1), :], block, NT, preferred_element_type=F32
            )
            for j in range(4):
                b = 4 * i + j
                c = cosb[y, b : b + 1, :]
                d = sinb[y, b : b + 1, :]
                tre = terms[j * 128 : j * 128 + 64]
                tim = terms[j * 128 + 64 : (j + 1) * 128]
                re = re + (c * tre - d * tim)
                im = im + (d * tre + c * tim)
        pat = jnp.concatenate([re, im], axis=0).astype(BF16)
        pat = jnp.dot(perm, pat, preferred_element_type=F32)
        for h in range(2):
            send1[pl.ds((2 * y + h) * nbox, nbox)] = (
                pat[:, h * 128 : (h + 1) * 128].reshape(nbox, 8, 128).astype(BF16)
            )

        @pl.when(s == 0)
        def _():
            pl.semaphore_wait(barrier, total - 1)
            to_sibling.start()

        def send(g, j):
            pltpu.make_async_remote_copy(
                src_ref=send1.at[j * nbox + g],
                dst_ref=recv1.at[rank],
                send_sem=s1,
                recv_sem=r1,
                device_id=g * ndir + j,
                device_id_type=LOGICAL,
            ).start()

        for g in groups[:-1]:
            for h in range(2):
                send(g, 2 * y + h)
        for h in range(2):
            j = 2 * y + h

            @pl.when(j != me)
            def _():
                send(box, j)

            @pl.when(j == me)
            def _():
                own1.start()

        return carry

    lax.fori_loop(0, chips, pattern_step, 0)

    to_other.start()

    def all_but_one(there, here, send_sem, recv_sem):
        return pltpu.make_async_remote_copy(
            src_ref=there.at[pl.ds(0, total - 1)],
            dst_ref=here.at[pl.ds(0, total - 1)],
            send_sem=send_sem,
            recv_sem=recv_sem,
            device_id=lax.rem(rank + 1, total),
            device_id_type=LOGICAL,
        )

    def near_box(x, own, b):
        count = ncount[b]
        gathered = jnp.concatenate(
            [
                x[jnp.where(k < count, nlist[k, b] - rank * boxes + own, boxes + half)]
                for k in range(8)
            ],
            axis=0,
        )
        zr = jnp.concatenate([zbuf[b, k, :, 0:128] for k in range(8)], axis=1)
        zi = jnp.concatenate([zbuf[b, k, :, 128:256] for k in range(8)], axis=1)
        both = jnp.dot(
            jnp.concatenate([zr, zi], axis=0), gathered, preferred_element_type=F32
        )
        cross = pltpu.roll(both[128:256], 64, 1)
        lane = lax.broadcasted_iota(jnp.int32, (128, 128), 1)
        near[b] = both[0:128] + jnp.where(lane < 64, -cross, cross)

    def near_sibling(i, carry):
        near_box(xsib, core * half, (1 - core) * half + i)
        return carry

    for table in tables:
        table.wait()
    slots = src.shape[0]
    nothing = tr_hbm.shape[0]

    def live_step(t, carry):
        for k in range(slots):
            op[k, t] = jnp.where(k < used[t], off[k, t], nothing)
        return carry

    lax.fori_loop(0, total, live_step, 0, unroll=4)
    load_z.wait()
    to_sibling.wait_recv()
    lax.fori_loop(0, half, near_sibling, 0)

    load_t.wait()
    own1.wait()
    all_but_one(send1, recv1, s1, r1).wait_recv()

    own2 = pltpu.make_async_copy(send2.at[rank], recv2.at[me * nbox + box], own_sem.at[1])
    sign = jnp.where(lax.broadcasted_iota(jnp.int32, (8, 128), 0) < 4, -1.0, 1.0)

    def group_of(s):
        code = sum(
            jnp.where(s == i, z * side + x, 0) for i, (z, x) in enumerate(far_groups(side))
        )
        return group_at((code // side, lax.rem(code, side)))

    def translate_group(s):
        g = group_of(s)
        for i in range(ndir):
            t = g * ndir + i
            straight = jnp.zeros((8, 128), F32)
            crossed = jnp.zeros((8, 128), F32)
            for k in range(slots):
                v = recv1[src[k, t]].astype(F32)
                tau = trans[op[k, t]]
                straight = straight + tau[0:1] * v
                crossed = crossed + tau[1:2] * v
            total_in = straight + sign * pltpu.roll(crossed, 4, 0)
            send2[t] = total_in.astype(BF16)

            @pl.when(t != rank)
            def _():
                pltpu.make_async_remote_copy(
                    src_ref=send2.at[t],
                    dst_ref=recv2.at[me * nbox + box],
                    send_sem=s2,
                    recv_sem=r2,
                    device_id=t,
                    device_id_type=LOGICAL,
                ).start()

            @pl.when(t == rank)
            def _():
                own2.start()


    def translate_step(s, carry):
        translate_group(s)
        return carry

    def near_other(i, carry):
        near_box(xoth, (1 - core) * half, core * half + i)
        return carry

    lax.fori_loop(0, nbox, translate_step, 0)
    to_other.wait_recv()
    lax.fori_loop(0, half, near_other, 0)

    own2.wait()
    all_but_one(send2, recv2, s2, r2).wait_recv()

    for y in range(chips):
        pair = jnp.concatenate(
            [
                recv2[(2 * y + h) * nbox : (2 * y + h + 1) * nbox]
                .astype(F32)
                .reshape(128, 128)
                .astype(BF16)
                for h in range(2)
            ],
            axis=1,
        )
        inc[:, y * 256 : (y + 1) * 256] = jnp.dot(perm_t, pair, preferred_element_type=F32)

    for i in range(boxes // 4):
        for j in range(4):
            b = 4 * i + j
            for y in range(chips):
                lanes = slice(y * 256, (y + 1) * 256)
                c = cosb[y, b : b + 1, :]
                d = sinb[y, b : b + 1, :]
                re = inc[0:64, lanes]
                im = inc[64:128, lanes]
                shf[i, j * 128 : j * 128 + 64, lanes] = (c * re + d * im).astype(BF16)
                shf[i, j * 128 + 64 : (j + 1) * 128, lanes] = (c * im - d * re).astype(BF16)
        mixed = jnp.dot(shf[i], a_ref[...], preferred_element_type=F32)
        for j in range(4):
            b = 4 * i + j
            m = mixed[j * 128 : (j + 1) * 128]
            far = jnp.concatenate(
                [m[0:64, 0:128] + m[64:128, 128:256], m[64:128, 0:128] - m[0:64, 128:256]], axis=0
            )
            out[b] = (near[b] + far.T).astype(BF16)

    to_sibling.wait_send()
    to_other.wait_send()
    all_but_one(send1, recv1, s1, r1).wait_send()
    all_but_one(send2, recv2, s2, r2).wait_send()


def local(
    nbox,
    ndir,
    currents,
    near_blocks,
    near_list,
    near_count,
    radiation,
    child_angle,
    translation,
    inter_src,
    inter_off,
    inter_count,
):
    boxes = currents.shape[0]
    total = nbox * ndir
    hbm = pl.BlockSpec(memory_space=pltpu.HBM)
    dma = pltpu.SemaphoreType.DMA
    return pl.pallas_call(
        functools.partial(kernel, nbox, ndir),
        out_shape=pltpu.VMEM((boxes, 128, 128), BF16),
        in_specs=[hbm] * 10,
        out_specs=pl.BlockSpec(memory_space=pltpu.VMEM),
        scratch_shapes=[
            pltpu.SMEM(near_list.shape[::-1], jnp.int32),
            pltpu.SMEM(near_count.shape, jnp.int32),
            pltpu.SMEM(inter_src.shape[::-1], jnp.int32),
            pltpu.SMEM(inter_off.shape[::-1], jnp.int32),
            pltpu.SMEM(inter_count.shape, jnp.int32),
            pltpu.SMEM(inter_off.shape[::-1], jnp.int32),
            pltpu.VMEM((3 * boxes // 2 + 1, 128, 128), BF16),
            pltpu.VMEM((3 * boxes // 2 + 1, 128, 128), BF16),
            pltpu.VMEM(near_blocks.shape, BF16),
            pltpu.VMEM(radiation.shape, BF16),
            pltpu.VMEM(child_angle.shape, F32),
            pltpu.VMEM((translation.shape[0] + 4, 2, 128), F32),
            pltpu.VMEM((ndir // 2, boxes, 256), F32),
            pltpu.VMEM((ndir // 2, boxes, 256), F32),
            pltpu.VMEM((boxes * 128, 256), BF16),
            pltpu.VMEM((total, 8, 128), BF16),
            pltpu.VMEM((total, 8, 128), BF16),
            pltpu.VMEM((total, 8, 128), BF16),
            pltpu.VMEM((total, 8, 128), BF16),
            pltpu.VMEM((boxes, 128, 128), F32),
            pltpu.VMEM((128, ndir * 128), F32),
            pltpu.VMEM((boxes // 4, 512, ndir * 128), BF16),
            dma((6,)),
            dma((5,)),
            dma((2,)),
            dma,
            dma,
            dma,
            dma,
            dma((2,)),
            dma((2,)),
        ],
        compiler_params=pltpu.CompilerParams(
            collective_id=0, has_side_effects=True, vmem_limit_bytes=57 * 2**20
        ),
    )(
        near_list.T,
        near_count,
        inter_src.T,
        inter_off.T,
        inter_count,
        currents,
        near_blocks,
        radiation,
        child_angle,
        translation,
    )


def solution(mesh):
    nbox, ndir = mesh.shape["box"], mesh.shape["dir"]
    return jax.shard_map(
        functools.partial(local, nbox, ndir),
        mesh=mesh,
        in_specs=(
            P(("box", "dir"), None, None),
            P(("box", "dir"), None, None, None),
            P(("box", "dir"), None),
            P(("box", "dir")),
            P(),
            P(("box", "dir"), None),
            P(),
            P(),
            P(),
            P(),
        ),
        out_specs=P(("box", "dir"), None, None),
        check_vma=False,
    )
```
